512 devices in a mesh: blk: 128 (over z, y, core), col: 4 (over x).
Axes of the slice: x: 4, y: 8, z: 8, core: 2. Of those that a mesh axis runs over, the one named last changes fastest.
Arguments:
- coords: float32 [1024, 2, 128], P('blk'), may hold values from -0.125 to 1.125, as said below
- neighbours: int32 [1024, 4], P('blk'), may hold values from -1 to 1023, as said below
- sections: int32 [1024], P('blk'), may hold values from 0 to 7, as said below
- normals: float32 [16, 131072], P('col', 'blk'), may hold values from -6 to 6
Outputs:
- samples: float32 [16, 131072], P('col', 'blk')
The draws below stay inside these ranges and needn't reach their ends.
Inputs may be any that keep to these rules, and one draw needn't show every extreme that they name: `neighbours`: every listed block has a lower section than the block that lists it; no block is listed twice in one row; blocks of section 0 list -1 only, other blocks list -1 only where fewer than 4 blocks of lower section exist. `sections`: among the 8 blocks of one device at most 2 share a section, and on every device exactly 2 do. `coords`: the points of one block lie in a small square around a centre in the unit square.
All inputs are finite; a program needn't handle non-finite values.
Results may differ from the reference program's by a relative error of at most 0.0003.
Values sent between devices are 32-bit elements; how exact they have to be, the bound alone decides.
A program may use at most 64 MiB of HBM per device.

```python
import jax
import jax.numpy as jnp
from jax import lax

B = 128
K = 4
SECTIONS = 8
BLK_DEV = 8
CAP = 2
NB = 1024
COLS = 16
NLOC = 131072


def section_lookup(key):
    relabel_key, shuffle_key = jax.random.split(key)
    devices = NB // BLK_DEV
    slots = jnp.arange(BLK_DEV)
    labels = jnp.where(slots < CAP, 0, 1 + (slots - CAP) % (SECTIONS - 1))
    relabel = jax.vmap(lambda one_key: jax.random.permutation(one_key, SECTIONS))(jax.random.split(relabel_key, devices))
    section_grid = relabel[:, labels]
    section_grid = jax.vmap(lambda one_key, row_now: jax.random.permutation(one_key, row_now))(jax.random.split(shuffle_key, devices), section_grid)
    return section_grid.reshape(NB).astype(jnp.int32)


def draw_sections(key, part):
    return section_lookup(key)


def draw_neighbours(key, part):
    section_now = section_lookup(key)
    key = jax.random.fold_in(key, 23)
    scores = jax.random.randint(key, (NB, NB), 0, 4096) * NB + jnp.arange(NB)[None, :]
    allowed = section_now[None, :] < section_now[:, None]
    scores = jnp.where(allowed, scores, -1)
    chosen, _ = lax.top_k(scores, K)
    return jnp.where(chosen >= 0, chosen % NB, -1).astype(jnp.int32)


def draw_coords(key, part):
    key = jax.random.fold_in(key, 11)
    centre_key, offset_key = jax.random.split(key)
    centre = jax.random.uniform(centre_key, (NB, 2, 1), jnp.float32)
    spread = 0.125
    offsets = jax.random.uniform(offset_key, (NB, 2, B), jnp.float32, -spread, spread)
    return (centre + offsets).astype(jnp.float32)


def block_levels(stream_key, extent, shards, low, largest):
    def one(axis_at, blocks):
        draws = jax.random.uniform(jax.random.fold_in(jax.random.fold_in(stream_key, 6), axis_at), (blocks,), jnp.float32, low / len(shards), largest / len(shards))
        return jnp.repeat(jnp.exp(draws), extent[axis_at] // blocks).reshape((-1,) + (1,) * (len(extent) - axis_at - 1))

    loudness = one(*shards[0])
    for cut in shards[1:]:
        loudness = loudness * one(*cut)
    return loudness


def centred(own_key, extent, deviation, limit, shards=(), kind=jnp.bfloat16):
    values = deviation * jax.random.normal(own_key, extent, jnp.float32)
    if shards:
        values = values * block_levels(own_key, extent, shards, -0.22, 0.18)
    return jnp.clip(values, -limit, limit).astype(kind)


def setup_inputs(seed: int = 0) -> dict:
    seeds = jax.random.split(jax.random.key(seed), 5)
    return {
        "coords": draw_coords(jax.random.fold_in(seeds[4], 71), 0),
        "neighbours": draw_neighbours(jax.random.fold_in(seeds[4], 71), 0),
        "sections": draw_sections(jax.random.fold_in(seeds[4], 71), 0),
        "normals": centred(seeds[3], (COLS, NLOC), 1.0, 6.0, ((0, 4), (1, 128)), jnp.float32),
    }


length_scale = 0.5
nugget_var = 0.1

def covariance_kernel(left_pts, right_pts):
    delta_x = left_pts[0][:, None] - right_pts[0][None, :]
    delta_y = left_pts[1][:, None] - right_pts[1][None, :]
    return jnp.exp(-jnp.sqrt(delta_x * delta_x + delta_y * delta_y) / length_scale)

def factor(own_pts, near_pts, present):
    points = own_pts.shape[1]
    near_cov = covariance_kernel(near_pts, near_pts) * (present[:, None] * present[None, :])
    near_cov = near_cov + jnp.diag(nugget_var * present + (1.0 - present))
    cross_cov = covariance_kernel(own_pts, near_pts) * present[None, :]
    self_cov = covariance_kernel(own_pts, own_pts) + nugget_var * jnp.eye(points, dtype=jnp.float32)
    chol_near = jnp.linalg.cholesky(near_cov)
    whitened = lax.linalg.triangular_solve(chol_near, cross_cov.T, left_side=True, lower=True)
    cond_cov = self_cov - jnp.dot(whitened.T, whitened, precision=lax.Precision.HIGHEST)
    weight_t = lax.linalg.triangular_solve(chol_near, whitened, left_side=True, lower=True, transpose_a=True)
    return (weight_t.T, jnp.linalg.cholesky(cond_cov))

def reference(coords, neighbours, sections, normals):
    block_total = coords.shape[0]
    points = coords.shape[2]
    columns = normals.shape[0]
    block_order = jnp.argsort(sections, stable=True).astype(jnp.int32)
    white_noise = normals.reshape(columns, block_total, points)
    samples = jnp.zeros((columns, block_total, points), jnp.float32)

    def advance(samples, block_id):
        near_ids = neighbours[block_id]
        present_k = near_ids >= 0
        safe_ids = jnp.maximum(near_ids, 0).astype(jnp.int32)
        near_pts = jnp.where(present_k[:, None, None], coords[safe_ids], jnp.float32(0.0))
        near_pts = jnp.transpose(near_pts, (1, 0, 2)).reshape(2, K * points)
        present = jnp.repeat(present_k.astype(jnp.float32), points)
        weight, chol_self = factor(coords[block_id], near_pts, present)
        near_vals = samples[:, safe_ids, :] * present_k.astype(jnp.float32)[None, :, None]
        near_vals = near_vals.reshape(columns, K * points)
        updated = jnp.dot(near_vals, weight.T, precision=lax.Precision.HIGHEST)
        updated = updated + jnp.dot(white_noise[:, block_id, :], chol_self.T, precision=lax.Precision.HIGHEST)
        samples = samples.at[:, block_id, :].set(updated)
        return (samples, None)
    samples, _ = lax.scan(advance, samples, block_order)
    return samples.reshape(columns, block_total * points)
```

```python
import jax
import jax.numpy as jnp
from jax import lax
from jax.experimental import pallas as pl
from jax.experimental.pallas import tpu as pltpu
from jax.sharding import PartitionSpec as P

K = 4
SECTIONS = 8
CAP = 2
B = 128
ROUNDS = SECTIONS - 1
LINE = 8
ZERO_TILE = ROUNDS * 2 * LINE * CAP

length_scale = 0.5
nugget_var = 0.1

HIGHEST = lax.Precision.HIGHEST
F32 = jnp.float32
BF16 = jnp.bfloat16


def iota(shape, dim):
    return lax.broadcasted_iota(jnp.int32, shape, dim)


def place():
    blk = lax.axis_index("blk")
    core = blk % 2
    y = (blk // 2) % LINE
    z = blk // (2 * LINE)
    along = (1 - core) * z + core * y
    across = (1 - core) * y + core * z
    return core, along, across


def device_at(core, along, across, other_core):
    chip = (1 - core) * (along * LINE + across) + core * (across * LINE + along)
    return chip * 2 + other_core


def line_targets(core, along, across):
    same = [
        (device_at(core, (along + d) % LINE, across, core), 2 * along + core) for d in range(1, LINE)
    ]
    other = [
        (device_at(core, along, (across + d) % LINE, 1 - core), 2 * across + core) for d in range(LINE)
    ]
    return same + other


def line_sources(core, along, across):
    same = [device_at(core, (along + d) % LINE, across, core) for d in range(1, LINE)]
    other = [device_at(core, (along + d) % LINE, across, 1 - core) for d in range(LINE)]
    return same + other


def cross_peers(core, along, across):
    return [
        (device_at(core, along, (across + d) % LINE, core), (across + d) % LINE) for d in range(1, LINE)
    ]


def greet(core, along, across):
    barrier = pltpu.get_barrier_semaphore()
    col = lax.axis_index("col")
    cols = lax.axis_size("col")
    count = 0
    for device in line_sources(core, along, across):
        pl.semaphore_signal(barrier, inc=1, device_id={"blk": device}, device_id_type=pl.DeviceIdType.MESH)
        count += 1
    for device, _ in cross_peers(core, along, across):
        pl.semaphore_signal(barrier, inc=1, device_id={"blk": device}, device_id_type=pl.DeviceIdType.MESH)
        count += 1
    for d in range(1, cols):
        pl.semaphore_signal(
            barrier, inc=1, device_id={"col": (col + d) % cols}, device_id_type=pl.DeviceIdType.MESH
        )
        count += 1
    pl.semaphore_wait(barrier, count)


def remote(src, dst, send_sem, recv_sem, device_id):
    return pltpu.make_async_remote_copy(
        src_ref=src,
        dst_ref=dst,
        send_sem=send_sem,
        recv_sem=recv_sem,
        device_id=device_id,
        device_id_type=pl.DeviceIdType.MESH,
    )


def wait_bytes(ref, sem):
    pltpu.make_async_copy(ref, ref, sem).wait()


def exchange_kernel(
    slot_ref,
    coords_ref,
    code_ref,
    ids_ref,
    asked_ref,
    normals_ref,
    near_ref,
    key_ref,
    draws_ref,
    own_a,
    own_b,
    own_n,
    got_a,
    got_b,
    got_n,
    picked,
    got_p,
    send_sems,
    recv_sems,
):
    core, along, across = place()
    col = lax.axis_index("col")
    cols = lax.axis_size("col")
    my_slot = 2 * along + core
    own_a[0] = coords_ref[:, 0, :]
    own_a[1] = coords_ref[:, 1, :]
    own_a[2] = code_ref[...]
    own_b[0] = ids_ref[...]
    own_b[1] = asked_ref[...]
    for owner in range(cols):
        for half in range(2):
            slot = slot_ref[owner + half * cols]
            drawn = jnp.zeros((4, B), F32)
            for at in range(LINE):
                drawn = drawn + normals_ref[:, at * B : (at + 1) * B] * (slot == at).astype(F32)
            own_n[owner, half * 4 : half * 4 + 4, :] = drawn
    greet(core, along, across)
    for device, slot in line_targets(core, along, across):
        remote(own_a, got_a.at[slot], send_sems.at[0], recv_sems.at[0], {"blk": device}).start()
    for device, _ in cross_peers(core, along, across):
        remote(own_b, got_b.at[across], send_sems.at[1], recv_sems.at[1], {"blk": device}).start()
    for d in range(1, cols):
        to = (col + d) % cols
        remote(own_n.at[to], got_n.at[col], send_sems.at[2], recv_sems.at[2], {"col": to}).start()
    got_a[my_slot] = own_a[...]
    got_b[across] = own_b[...]
    got_n[col] = own_n[col]
    lane = iota((1, B), 1)
    lane_dev = device_at(core, lane // (2 * LINE), across, (lane // LINE) % 2)
    lane_block = lane_dev * LINE + lane % LINE
    sub = iota((LINE, B), 0)
    entry_half = (iota((1, B), 1) // K) % 2
    wait_bytes(got_a.at[pl.ds(0, 2 * LINE - 1)], recv_sems.at[0])
    wait_bytes(got_b.at[pl.ds(0, LINE - 1)], recv_sems.at[1])
    chosen = jnp.concatenate(
        [(got_b[peer, 0] == lane_block).astype(F32) for peer in range(LINE)], axis=0
    )
    for axis in range(2):
        held = got_a[:, axis].reshape(B, B)
        moved = jnp.dot(chosen, held, precision=HIGHEST, preferred_element_type=F32)
        picked[:, axis] = moved.reshape(LINE, LINE, B)
    for device, peer in cross_peers(core, along, across):
        remote(picked.at[peer], got_p.at[across], send_sems.at[3], recv_sems.at[3], {"blk": device}).start()
    got_p[across] = picked[across]
    sums = [jnp.zeros((LINE, B), jnp.int32) for _ in range(LINE)]
    for dev in range(2 * LINE):
        block = device_at(core, dev // 2, across, dev % 2) * LINE + sub
        value = got_a[dev, 2].astype(jnp.int32) + (2 * dev + 1)
        for peer in range(LINE):
            sums[peer] = sums[peer] + jnp.where(block == got_b[peer, 1], value, 0)
    for peer in range(LINE):
        total = jnp.sum(sums[peer], axis=0, keepdims=True)
        value = total - 1
        turned = value + entry_half * (1 - 2 * (value % 2))
        key_ref[peer : peer + 1, :] = jnp.where(total > 0, turned, ZERO_TILE)
    wait_bytes(got_n.at[pl.ds(0, cols - 1)], recv_sems.at[2])
    draws_ref[...] = got_n[...]
    wait_bytes(got_p.at[pl.ds(0, LINE - 1)], recv_sems.at[3])
    for axis in range(2):
        near = got_p[0, axis]
        for peer in range(1, LINE):
            near = near + got_p[peer, axis]
        near_ref[axis] = near
    wait_bytes(got_a.at[pl.ds(0, 2 * LINE - 1)], send_sems.at[0])
    wait_bytes(got_b.at[pl.ds(0, LINE - 1)], send_sems.at[1])
    wait_bytes(got_n.at[pl.ds(0, cols - 1)], send_sems.at[2])
    wait_bytes(got_p.at[pl.ds(0, LINE - 1)], send_sems.at[3])


def split3(x):
    high = x.astype(BF16).astype(F32)
    rest = x - high
    middle = rest.astype(BF16).astype(F32)
    return high, middle, rest - middle


def thin_product(left, right):
    l1, l2, l3 = split3(left)
    r1, r2, r3 = split3(right)
    tall_left = jnp.concatenate([l1, l1, l2, l2, l1, l3], axis=0).astype(BF16)
    tall_right = jnp.concatenate([r1, r2, r1, r2, r3, r1], axis=0).astype(BF16)
    return lax.dot_general(tall_left, tall_right, (((0,), (0,)), ((), ())), preferred_element_type=F32)


def spread(tile, first):
    return [jnp.broadcast_to(tile[:, first + j : first + j + 1], (8, B)) for j in range(8)]


def weighted_rows(factors, rows):
    terms = [factors[j] * rows[j : j + 1, :] for j in range(8)]
    return ((terms[0] + terms[1]) + (terms[2] + terms[3])) + ((terms[4] + terms[5]) + (terms[6] + terms[7]))


def eliminate(rows, columns, sub):
    columns = list(columns)
    full = rows
    scales = []
    for j in range(8):
        below, here = sub > j, sub == j
        pivot = columns[j][j : j + 1, :]
        inverse = 1.0 / pivot
        factors = columns[j] * inverse
        under = jnp.where(below, factors, 0.0)
        scaled = full[j : j + 1, :] * inverse
        full = jnp.where(here, scaled, full - columns[j] * scaled)
        rows = rows - under * rows[j : j + 1, :]
        for later in range(j + 1, 8):
            columns[later] = jnp.where(
                here, columns[later] * inverse, columns[later] - factors * columns[later][j : j + 1, :]
            )
        scales.append(lax.rsqrt(pivot))
    scale = scales[7]
    for j in range(7):
        scale = jnp.where(sub == j, scales[j], scale)
    return rows * scale, full


def inverse_factors(matrices):
    sub, lane = iota((8, B), 0), iota((8, B), 1)
    wide = iota((B, B), 1)
    matrices = list(matrices)
    ahead = [m[0:8] for m in matrices]
    panels = [[] for _ in matrices]
    for panel in range(B // 8):
        at = 8 * panel
        inside = (lane >= at) & (lane < at + 8)
        for q in range(len(matrices)):
            unit = jnp.where(lane == sub + at, 1.0, 0.0)
            done, full = eliminate(jnp.where(inside, unit, ahead[q]), spread(ahead[q], at), sub)
            panels[q].append(jnp.where(lane < at + 8, done, 0.0))
            if at + 8 < B:
                following = matrices[q][at + 8 : at + 16]
                ahead[q] = jnp.where(inside, 0.0, following) - weighted_rows(spread(following, at), full)
                kept = jnp.where((wide >= at) & (wide < at + 8), 0.0, matrices[q])
                matrices[q] = kept - thin_product(done, done)
    return [jnp.concatenate(p, axis=0) for p in panels]


def factor_rows(rows, columns, sub):
    columns = list(columns)
    scales = []
    for j in range(8):
        below = sub > j
        pivot = columns[j][j : j + 1, :]
        inverse = 1.0 / pivot
        factors = jnp.where(below, columns[j] * inverse, 0.0)
        rows = rows - factors * rows[j : j + 1, :]
        for later in range(j + 1, 8):
            columns[later] = columns[later] - factors * columns[later][j : j + 1, :]
        scales.append(lax.rsqrt(pivot))
    scale = scales[7]
    for j in range(7):
        scale = jnp.where(sub == j, scales[j], scale)
    return rows * scale


def upper_cholesky(matrices):
    sub, lane = iota((8, B), 0), iota((8, B), 1)
    matrices = list(matrices)
    ahead = [m[0:8] for m in matrices]
    panels = [[] for _ in matrices]
    for panel in range(B // 8):
        at = 8 * panel
        for q in range(len(matrices)):
            rows = ahead[q]
            done = factor_rows(rows, spread(rows, at), sub)
            done = jnp.where(lane >= sub + at, done, 0.0)
            panels[q].append(done)
            if at + 8 < B:
                following = matrices[q][at + 8 : at + 16]
                turned = done[:, at + 8 : at + 16].T
                factors = [jnp.broadcast_to(turned[:, j : j + 1], (8, B)) for j in range(8)]
                ahead[q] = following - weighted_rows(factors, done)
                matrices[q] = matrices[q] - thin_product(done, done)
    return [jnp.concatenate(p, axis=0) for p in panels]


def multiply(left, right):
    return jnp.dot(left, right, precision=HIGHEST, preferred_element_type=F32)


def multiply_tn(left, right):
    return lax.dot_general(
        left, right, (((0,), (0,)), ((), ())), precision=HIGHEST, preferred_element_type=F32
    )


def covariance(row_x, row_y, col_x, col_y):
    dx = col_x - row_x
    dy = col_y - row_y
    return jnp.exp(-jnp.sqrt(dx * dx + dy * dy) / length_scale)


def factor_kernel(slot_ref, there_ref, coords_ref, near_ref, draws_ref, weight_ref, noise_ref, cov, inverses):
    eye = (iota((B, B), 0) == iota((B, B), 1)).astype(F32)
    for q in range(2):
        own = coords_ref[slot_ref[q]]
        points = [
            (near_ref[0, q * K + k : q * K + k + 1, :], near_ref[1, q * K + k : q * K + k + 1, :])
            for k in range(K)
        ] + [(own[0:1], own[1:2])]
        there = [there_ref[q * K + k].astype(F32) for k in range(K)] + [jnp.float32(1.0)]
        for a in range(K + 1):
            col_x = jnp.broadcast_to(points[a][0], (B, B)).T
            col_y = jnp.broadcast_to(points[a][1], (B, B)).T
            for b in range(a, K + 1):
                block = covariance(points[b][0], points[b][1], col_x, col_y) * (there[a] * there[b])
                if a == b:
                    block = block + (nugget_var * there[a] + (1.0 - there[a])) * eye
                cov[q, a, :, b * B : (b + 1) * B] = block

    def step(k, carry):
        start = pl.multiple_of(k * B, B)
        inverse = inverse_factors([cov[q, k, :, pl.ds(start, B)] for q in range(2)])
        for q in range(2):
            inverses[q, k] = inverse[q]
        for at in range(K):

            @pl.when(k == at)
            def _(at=at):
                for q in range(2):
                    rest = slice((at + 1) * B, (K + 1) * B)
                    white = multiply(inverse[q], cov[q, at, :, rest])
                    cov[q, at, :, rest] = white
                    for row in range(at + 1, K + 1):
                        first = (row - at - 1) * B
                        cov[q, row, :, row * B :] = cov[q, row, :, row * B :] - multiply_tn(
                            white[:, first : first + B], white[:, first:]
                        )

        return carry

    lax.fori_loop(0, K, step, 0)
    for q in range(2):
        for k in reversed(range(K)):
            total = cov[q, k, :, K * B :]
            if k + 1 < K:
                total = total - multiply(cov[q, k, :, (k + 1) * B : K * B], weight_ref[q, (k + 1) * B :, :])
            weight_ref[q, k * B : (k + 1) * B, :] = multiply_tn(inverses[q, k], total)
    upper = upper_cholesky([cov[q, K, :, K * B :] for q in range(2)])
    rows = draws_ref.shape[0] * draws_ref.shape[1]
    noise = jnp.dot(
        draws_ref[...].reshape(rows, B),
        jnp.concatenate(upper, axis=1),
        precision=HIGHEST,
        preferred_element_type=F32,
    )
    half = (iota((rows, B), 0) // 4) % 2
    noise_ref[...] = jnp.where(half == 0, noise[:, :B], noise[:, B:]).reshape(noise_ref.shape)


def section_kernel(
    key_ref,
    rank_ref,
    out_key_ref,
    weight_ref,
    noise_ref,
    out_ref,
    early,
    late,
    got_noise,
    values,
    turned,
    got_line,
    held,
    picked,
    got_cross,
    high,
    low,
    local_sem,
    wave_send,
    wave_recv,
    line_send,
    line_recv,
    cross_send,
    cross_recv,
):
    core, along, across = place()
    col = lax.axis_index("col")
    cols = lax.axis_size("col")
    my_slot = 2 * along + core
    sub = iota((8, B), 0)
    held[ZERO_TILE] = jnp.zeros((8, B), F32)
    greet(core, along, across)
    peers = [(col + d) % cols for d in range(1, cols)]
    for to in peers:
        remote(noise_ref.at[to], got_noise.at[col], wave_send.at[0], wave_recv.at[0], {"col": to}).start()
    for wave, buffer in ((0, early), (1, late)):
        for to in peers:
            remote(
                weight_ref.at[wave], buffer.at[col], wave_send.at[1 + wave], wave_recv.at[1 + wave], {"col": to}
            ).start()
        pltpu.make_async_copy(weight_ref.at[wave], buffer.at[col], local_sem.at[wave]).start()
    got_noise[col] = noise_ref[col]

    def noise_of(section):
        tiles = []
        for slot in range(CAP):
            rank = rank_ref[CAP * section + slot]
            tile = got_noise[rank % cols]
            swapped = pltpu.roll(tile, 4, 0)
            keep = (rank // cols == slot).astype(F32)
            tiles.append(tile * keep + swapped * (1.0 - keep))
        return jnp.where(sub < 4, tiles[0], tiles[1])

    def spread_values(s, tile):
        values[s] = tile
        turned[CAP * s] = tile
        turned[CAP * s + 1] = pltpu.roll(tile, 4, 0)

    def prepare(section, both):
        for slot in range(CAP):
            rank = rank_ref[CAP * section + slot]
            place_in_wave = rank % cols
            weight = early[place_in_wave]
            if both:
                is_late = (rank // cols).astype(F32)
                weight = weight * (1.0 - is_late) + late[place_in_wave] * is_late
            part = weight.astype(BF16)
            high[:, slot * B : (slot + 1) * B] = part
            low[:, slot * B : (slot + 1) * B] = (weight - part.astype(F32)).astype(BF16)

    def share(s):
        for device, slot in line_targets(core, along, across):
            remote(
                values.at[s], got_line.at[s, slot], line_send.at[s], line_recv.at[s], {"blk": device}
            ).start()
        got_line[s, my_slot] = values[s]

    def pass_on(s):
        wait_bytes(got_line.at[s, pl.ds(0, 2 * LINE - 1)], line_recv.at[s])
        first = s * (2 * LINE * CAP)
        for dev in range(2 * LINE):
            tile = got_line[s, dev]
            held[first + 2 * dev] = tile
            held[first + 2 * dev + 1] = pltpu.roll(tile, 4, 0)

        def pick(peer, slot_there):
            lanes = (s + 1) * (CAP * K)
            for k in range(K):
                upper = held[key_ref[peer, lanes + k]]
                lower = held[key_ref[peer, lanes + K + k]]
                slot_there[k] = jnp.where(sub < 4, upper, lower)

        for device, peer in cross_peers(core, along, across):
            pick(peer, picked.at[s, peer])
            remote(
                picked.at[s, peer], got_cross.at[s, across], cross_send.at[s], cross_recv.at[s], {"blk": device}
            ).start()
        pick(across, got_cross.at[s, across])

    def collect(s):
        wait_bytes(got_cross.at[s, pl.ds(0, LINE - 1)], cross_recv.at[s])
        near = []
        for k in range(K):
            tile = got_cross[s, 0, k]
            for peer in range(1, LINE):
                tile = tile + got_cross[s, peer, k]
            near.append(tile)
        near = jnp.concatenate(near, axis=1)
        part = near.astype(BF16).astype(F32)
        both = jnp.concatenate([part, near - part], axis=0).astype(BF16)
        first = jnp.dot(both, high[...], preferred_element_type=F32)
        second = jnp.dot(both[0:8], low[...], preferred_element_type=F32)
        total = first[0:8] + (first[8:16] + second)
        update = jnp.where(sub < 4, total[:, :B], total[:, B:])
        spread_values(s + 1, update + noise_of(s + 1))

    wait_bytes(got_noise.at[pl.ds(0, cols - 1)], wave_recv.at[0])
    spread_values(0, noise_of(0))
    share(0)
    pass_on(0)
    wait_bytes(early.at[pl.ds(0, cols - 1)], wave_recv.at[1])
    pltpu.make_async_copy(weight_ref.at[0], early.at[col], local_sem.at[0]).wait()
    prepare(1, False)
    collect(0)
    share(1)
    wait_bytes(late.at[pl.ds(0, cols - 1)], wave_recv.at[2])
    pltpu.make_async_copy(weight_ref.at[1], late.at[col], local_sem.at[1]).wait()

    def section(s, carry):
        prepare(s + 1, True)
        pass_on(s)
        collect(s)

        @pl.when(s + 1 < ROUNDS)
        def _():
            share(s + 1)

        return carry

    lax.fori_loop(1, ROUNDS, section, 0)
    for block in range(out_ref.shape[1] // B):
        out_ref[:, block * B : (block + 1) * B] = turned[out_key_ref[block]][0:4]
    wait_bytes(got_noise.at[pl.ds(0, cols - 1)], wave_send.at[0])
    wait_bytes(early.at[pl.ds(0, cols - 1)], wave_send.at[1])
    wait_bytes(late.at[pl.ds(0, cols - 1)], wave_send.at[2])

    def finish(s, carry):
        wait_bytes(got_line.at[s, pl.ds(0, 2 * LINE - 1)], line_send.at[s])
        wait_bytes(got_cross.at[s, pl.ds(0, LINE - 1)], cross_send.at[s])
        return carry

    lax.fori_loop(0, ROUNDS, finish, 0)


VMEM_SPEC = pl.BlockSpec(memory_space=pltpu.VMEM)
SMEM_SPEC = pl.BlockSpec(memory_space=pltpu.SMEM)
FACTOR_SCRATCH = [pltpu.VMEM((2, K + 1, B, (K + 1) * B), F32), pltpu.VMEM((2, K, B, B), F32)]
VMEM_LIMIT = 40 * 1024 * 1024


def local(coords, neighbours, sections, normals):
    blocks = coords.shape[0]
    cols = lax.axis_size("col")
    col = lax.axis_index("col")
    i32 = jnp.int32
    slots = jnp.arange(blocks, dtype=i32)
    same = sections[None, :] == sections[:, None]
    lower = sections[None, :] < sections[:, None]
    earlier = slots[None, :] < slots[:, None]
    within = jnp.sum((same & earlier).astype(i32), axis=1)
    rank = jnp.sum((lower | (same & earlier)).astype(i32), axis=1)
    by_rank = rank[None, :] == slots[:, None]
    slot_of_rank = jnp.sum(by_rank.astype(i32) * slots[None, :], axis=1)
    cells = jnp.arange(SECTIONS * CAP, dtype=i32)
    in_cell = cells[:, None] == (sections * CAP + within)[None, :]
    rank_of_cell = jnp.sum(in_cell.astype(i32) * rank[None, :], axis=1)
    listed = neighbours + 1
    asked = jnp.sum(in_cell.astype(i32)[:, :, None] * listed[None, :, :], axis=1).reshape(-1) - 1
    asked = jnp.pad(asked, (0, B - asked.shape[0]), constant_values=-1)
    mine = jnp.stack([col, col + cols])
    is_mine = rank[None, :] == mine[:, None]
    my_slots = jnp.sum(is_mine.astype(i32) * slots[None, :], axis=1)
    ids = jnp.sum(is_mine.astype(i32)[:, :, None] * listed[None, :, :], axis=1).reshape(-1) - 1
    there = (ids >= 0).astype(i32)
    code = (sections * (2 * LINE * CAP) + within).astype(F32)
    out_key = sections * CAP + within

    def tile(v):
        return jnp.broadcast_to(v[:, None], (blocks, B))

    shape = jax.ShapeDtypeStruct
    near, key, draws = pl.pallas_call(
        exchange_kernel,
        out_shape=(shape((2, 8, B), F32), shape((LINE, B), i32), shape((cols, 8, B), F32)),
        in_specs=[SMEM_SPEC] + [VMEM_SPEC] * 5,
        out_specs=(VMEM_SPEC,) * 3,
        scratch_shapes=[
            pltpu.VMEM((3, 8, B), F32),
            pltpu.VMEM((2, 8, B), i32),
            pltpu.VMEM((cols, 8, B), F32),
            pltpu.VMEM((2 * LINE, 3, 8, B), F32),
            pltpu.VMEM((LINE, 2, 8, B), i32),
            pltpu.VMEM((cols, 8, B), F32),
            pltpu.VMEM((LINE, 2, 8, B), F32),
            pltpu.VMEM((LINE, 2, 8, B), F32),
            pltpu.SemaphoreType.DMA((4,)),
            pltpu.SemaphoreType.DMA((4,)),
        ],
        compiler_params=pltpu.CompilerParams(
            collective_id=0, has_side_effects=True, vmem_limit_bytes=VMEM_LIMIT
        ),
        name="exchange",
    )(slot_of_rank, coords, tile(code), tile(ids), jnp.broadcast_to(asked[None, :], (8, B)), normals)

    weight, noise = pl.pallas_call(
        factor_kernel,
        out_shape=(shape((2, K * B, B), F32), shape((cols, 8, B), F32)),
        in_specs=[SMEM_SPEC] * 2 + [VMEM_SPEC] * 3,
        out_specs=(VMEM_SPEC,) * 2,
        scratch_shapes=FACTOR_SCRATCH,
        compiler_params=pltpu.CompilerParams(vmem_limit_bytes=VMEM_LIMIT),
        name="factor",
    )(my_slots, there, coords, near, draws)

    return pl.pallas_call(
        section_kernel,
        out_shape=shape(normals.shape, F32),
        in_specs=[SMEM_SPEC] * 3 + [VMEM_SPEC] * 2,
        out_specs=VMEM_SPEC,
        scratch_shapes=[
            pltpu.VMEM((cols, K * B, B), F32),
            pltpu.VMEM((cols, K * B, B), F32),
            pltpu.VMEM((cols, 8, B), F32),
            pltpu.VMEM((SECTIONS, 8, B), F32),
            pltpu.VMEM((SECTIONS * CAP, 8, B), F32),
            pltpu.VMEM((ROUNDS, 2 * LINE, 8, B), F32),
            pltpu.VMEM((ZERO_TILE + 1, 8, B), F32),
            pltpu.VMEM((ROUNDS, LINE, K, 8, B), F32),
            pltpu.VMEM((ROUNDS, LINE, K, 8, B), F32),
            pltpu.VMEM((K * B, CAP * B), BF16),
            pltpu.VMEM((K * B, CAP * B), BF16),
            pltpu.SemaphoreType.DMA((2,)),
            pltpu.SemaphoreType.DMA((3,)),
            pltpu.SemaphoreType.DMA((3,)),
            pltpu.SemaphoreType.DMA((ROUNDS,)),
            pltpu.SemaphoreType.DMA((ROUNDS,)),
            pltpu.SemaphoreType.DMA((ROUNDS,)),
            pltpu.SemaphoreType.DMA((ROUNDS,)),
        ],
        compiler_params=pltpu.CompilerParams(
            collective_id=1, has_side_effects=True, vmem_limit_bytes=VMEM_LIMIT
        ),
        name="sections",
    )(key, rank_of_cell, out_key, weight, noise)


def solution(mesh):
    in_specs = (P("blk", None, None), P("blk", None), P("blk"), P("col", "blk"))
    out_specs = P("col", "blk")
    return jax.shard_map(local, mesh=mesh, in_specs=in_specs, out_specs=out_specs, check_vma=False)
```

```python
import jax
import jax.numpy as jnp
from jax import lax
from jax.experimental import pallas as pl
from jax.experimental.pallas import tpu as pltpu
from jax.sharding import PartitionSpec as P

K = 4
SECTIONS = 8
CAP = 2
B = 128
ROUNDS = SECTIONS - 1
LINE = 8
ZERO_TILE = ROUNDS * 2 * LINE * CAP

length_scale = 0.5
nugget_var = 0.1

HIGHEST = lax.Precision.HIGHEST
F32 = jnp.float32
BF16 = jnp.bfloat16


def iota(shape, dim):
    return lax.broadcasted_iota(jnp.int32, shape, dim)


def place():
    blk = lax.axis_index("blk")
    core = blk % 2
    y = (blk // 2) % LINE
    z = blk // (2 * LINE)
    along = (1 - core) * z + core * y
    across = (1 - core) * y + core * z
    return core, along, across


def device_at(core, along, across, other_core):
    chip = (1 - core) * (along * LINE + across) + core * (across * LINE + along)
    return chip * 2 + other_core


FAR_FIRST = (4, 3, 5, 2, 6, 1, 7)


def line_targets(core, along, across):
    targets = []
    for d in FAR_FIRST + (0,):
        if d:
            targets.append((device_at(core, (along + d) % LINE, across, core), 2 * along + core))
        targets.append((device_at(core, along, (across + d) % LINE, 1 - core), 2 * across + core))
    return targets


def line_sources(core, along, across):
    same = [device_at(core, (along + d) % LINE, across, core) for d in range(1, LINE)]
    other = [device_at(core, (along + d) % LINE, across, 1 - core) for d in range(LINE)]
    return same + other


def cross_peers(core, along, across):
    return [
        (device_at(core, along, (across + d) % LINE, core), (across + d) % LINE) for d in FAR_FIRST
    ]


def greet(core, along, across):
    barrier = pltpu.get_barrier_semaphore()
    col = lax.axis_index("col")
    cols = lax.axis_size("col")
    mesh_id = pl.DeviceIdType.MESH
    sources = line_sources(core, along, across) + [device for device, _ in cross_peers(core, along, across)]
    for device in sources:
        pl.semaphore_signal(barrier, inc=1, device_id={"blk": device}, device_id_type=mesh_id)
    for d in range(1, cols):
        pl.semaphore_signal(barrier, inc=1, device_id={"col": (col + d) % cols}, device_id_type=mesh_id)
    return len(sources) + cols - 1


def await_answers(count):
    pl.semaphore_wait(pltpu.get_barrier_semaphore(), count)


def remote(src, dst, send_sem, recv_sem, device_id):
    return pltpu.make_async_remote_copy(
        src_ref=src,
        dst_ref=dst,
        send_sem=send_sem,
        recv_sem=recv_sem,
        device_id=device_id,
        device_id_type=pl.DeviceIdType.MESH,
    )


def wait_bytes(ref, sem):
    pltpu.make_async_copy(ref, ref, sem).wait()


def exchange_kernel(
    slot_ref,
    coords_ref,
    code_ref,
    ids_ref,
    asked_ref,
    normals_ref,
    near_ref,
    key_ref,
    draws_ref,
    own_a,
    own_b,
    own_n,
    got_a,
    got_b,
    got_n,
    picked,
    got_p,
    send_sems,
    recv_sems,
):
    core, along, across = place()
    answers = greet(core, along, across)
    col = lax.axis_index("col")
    cols = lax.axis_size("col")
    my_slot = 2 * along + core
    own_a[0] = coords_ref[:, 0, :]
    own_a[1] = coords_ref[:, 1, :]
    own_a[2] = code_ref[...]
    own_b[0] = ids_ref[...]
    own_b[1] = asked_ref[...]
    for owner in range(cols):
        for half in range(2):
            slot = slot_ref[owner + half * cols]
            drawn = jnp.zeros((4, B), F32)
            for at in range(LINE):
                drawn = drawn + normals_ref[:, at * B : (at + 1) * B] * (slot == at).astype(F32)
            own_n[owner, half * 4 : half * 4 + 4, :] = drawn
    await_answers(answers)
    for device, slot in line_targets(core, along, across):
        remote(own_a, got_a.at[slot], send_sems.at[0], recv_sems.at[0], {"blk": device}).start()
    for device, _ in cross_peers(core, along, across):
        remote(own_b, got_b.at[across], send_sems.at[1], recv_sems.at[1], {"blk": device}).start()
    for d in range(1, cols):
        to = (col + d) % cols
        remote(own_n.at[to], got_n.at[col], send_sems.at[2], recv_sems.at[2], {"col": to}).start()
    got_a[my_slot] = own_a[...]
    got_b[across] = own_b[...]
    got_n[col] = own_n[col]
    lane = iota((1, B), 1)
    lane_dev = device_at(core, lane // (2 * LINE), across, (lane // LINE) % 2)
    lane_block = lane_dev * LINE + lane % LINE
    sub = iota((LINE, B), 0)
    entry_half = (iota((1, B), 1) // K) % 2
    wait_bytes(got_a.at[pl.ds(0, 2 * LINE - 1)], recv_sems.at[0])
    wait_bytes(got_b.at[pl.ds(0, LINE - 1)], recv_sems.at[1])
    chosen = jnp.concatenate(
        [(got_b[peer, 0] == lane_block).astype(F32) for peer in range(LINE)], axis=0
    )
    for axis in range(2):
        held = got_a[:, axis].reshape(B, B)
        moved = jnp.dot(chosen, held, precision=HIGHEST, preferred_element_type=F32)
        picked[:, axis] = moved.reshape(LINE, LINE, B)
    for device, peer in cross_peers(core, along, across):
        remote(picked.at[peer], got_p.at[across], send_sems.at[3], recv_sems.at[3], {"blk": device}).start()
    got_p[across] = picked[across]
    sums = [jnp.zeros((LINE, B), jnp.int32) for _ in range(LINE)]
    for dev in range(2 * LINE):
        block = device_at(core, dev // 2, across, dev % 2) * LINE + sub
        value = got_a[dev, 2].astype(jnp.int32) + (2 * dev + 1)
        for peer in range(LINE):
            sums[peer] = sums[peer] + jnp.where(block == got_b[peer, 1], value, 0)
    for peer in range(LINE):
        total = jnp.sum(sums[peer], axis=0, keepdims=True)
        value = total - 1
        turned = value + entry_half * (1 - 2 * (value % 2))
        key_ref[peer : peer + 1, :] = jnp.where(total > 0, turned, ZERO_TILE)
    wait_bytes(got_n.at[pl.ds(0, cols - 1)], recv_sems.at[2])
    draws_ref[...] = got_n[...]
    wait_bytes(got_p.at[pl.ds(0, LINE - 1)], recv_sems.at[3])
    for axis in range(2):
        near = got_p[0, axis]
        for peer in range(1, LINE):
            near = near + got_p[peer, axis]
        near_ref[axis] = near
    wait_bytes(got_a.at[pl.ds(0, 2 * LINE - 1)], send_sems.at[0])
    wait_bytes(got_b.at[pl.ds(0, LINE - 1)], send_sems.at[1])
    wait_bytes(got_n.at[pl.ds(0, cols - 1)], send_sems.at[2])
    wait_bytes(got_p.at[pl.ds(0, LINE - 1)], send_sems.at[3])


def split3(x):
    high = x.astype(BF16).astype(F32)
    rest = x - high
    middle = rest.astype(BF16).astype(F32)
    return high, middle, rest - middle


def thin_product(left, right):
    l1, l2, l3 = split3(left)
    r1, r2, r3 = split3(right)
    tall_left = jnp.concatenate([l1, l1, l2, l2, l1, l3], axis=0).astype(BF16)
    tall_right = jnp.concatenate([r1, r2, r1, r2, r3, r1], axis=0).astype(BF16)
    return lax.dot_general(tall_left, tall_right, (((0,), (0,)), ((), ())), preferred_element_type=F32)


def spread(tile, first):
    return [jnp.broadcast_to(tile[:, first + j : first + j + 1], (8, B)) for j in range(8)]


def weighted_rows(factors, rows):
    terms = [factors[j] * rows[j : j + 1, :] for j in range(8)]
    return ((terms[0] + terms[1]) + (terms[2] + terms[3])) + ((terms[4] + terms[5]) + (terms[6] + terms[7]))


def eliminate(rows, columns, sub):
    columns = list(columns)
    full = rows
    scales = []
    for j in range(8):
        below, here = sub > j, sub == j
        pivot = columns[j][j : j + 1, :]
        inverse = 1.0 / pivot
        factors = columns[j] * inverse
        under = jnp.where(below, factors, 0.0)
        scaled = full[j : j + 1, :] * inverse
        full = jnp.where(here, scaled, full - columns[j] * scaled)
        rows = rows - under * rows[j : j + 1, :]
        for later in range(j + 1, 8):
            columns[later] = jnp.where(
                here, columns[later] * inverse, columns[later] - factors * columns[later][j : j + 1, :]
            )
        scales.append(lax.rsqrt(pivot))
    scale = scales[7]
    for j in range(7):
        scale = jnp.where(sub == j, scales[j], scale)
    return rows * scale, full


def panel_factors(matrices, inverted):
    sub, lane = iota((8, B), 0), iota((8, B), 1)
    wide = iota((B, B), 1)
    matrices = list(matrices)
    ahead = [m[0:8] for m in matrices]
    panels = [[] for _ in matrices]
    for panel in range(B // 8):
        at = 8 * panel
        inside = (lane >= at) & (lane < at + 8)
        for q in range(len(matrices)):
            rows, left = ahead[q], matrices[q]
            if inverted[q]:
                unit = jnp.where(lane == sub + at, 1.0, 0.0)
                done, full = eliminate(jnp.where(inside, unit, rows), spread(rows, at), sub)
                panels[q].append(jnp.where(lane < at + 8, done, 0.0))
            else:
                done, full = eliminate(rows, spread(rows, at), sub)
                panels[q].append(jnp.where(lane >= sub + at, done, 0.0))
            if at + 8 < B:
                following = left[at + 8 : at + 16]
                drop = weighted_rows(spread(following, at), full)
                if inverted[q]:
                    following = jnp.where(inside, 0.0, following)
                    left = jnp.where((wide >= at) & (wide < at + 8), 0.0, left)
                ahead[q] = following - drop
                matrices[q] = left - thin_product(done, done)
    return [jnp.concatenate(p, axis=0) for p in panels]


def multiply(left, right):
    return jnp.dot(left, right, precision=HIGHEST, preferred_element_type=F32)


def multiply_tn(left, right):
    return lax.dot_general(
        left, right, (((0,), (0,)), ((), ())), precision=HIGHEST, preferred_element_type=F32
    )


def covariance(row_x, row_y, col_x, col_y):
    dx = col_x - row_x
    dy = col_y - row_y
    return jnp.exp(-jnp.sqrt(dx * dx + dy * dy) / length_scale)


def build_covariances(slot_ref, there_ref, coords_ref, near_ref, cov):
    eye = (iota((B, B), 0) == iota((B, B), 1)).astype(F32)
    for q in range(2):
        own = coords_ref[slot_ref[q]]
        points = [
            (near_ref[0, q * K + k : q * K + k + 1, :], near_ref[1, q * K + k : q * K + k + 1, :])
            for k in range(K)
        ] + [(own[0:1], own[1:2])]
        there = [there_ref[q * K + k].astype(F32) for k in range(K)] + [jnp.float32(1.0)]
        for a in range(K + 1):
            col_x = jnp.broadcast_to(points[a][0], (B, B)).T
            col_y = jnp.broadcast_to(points[a][1], (B, B)).T
            for b in range(a, K + 1):
                block = covariance(points[b][0], points[b][1], col_x, col_y) * (there[a] * there[b])
                if a == b:
                    block = block + (nugget_var * there[a] + (1.0 - there[a])) * eye
                cov[q, a, :, b * B : (b + 1) * B] = block


def sample_kernel(
    key_ref,
    rank_ref,
    out_key_ref,
    slot_ref,
    there_ref,
    coords_ref,
    near_ref,
    draws_ref,
    out_ref,
    cov,
    inverses,
    weights,
    first_noise,
    noise,
    near_first,
    early,
    late,
    got_first,
    got_noise,
    got_near,
    values,
    turned,
    got_line,
    held,
    picked,
    got_cross,
    high,
    low,
    local_sem,
    col_send,
    col_recv,
    line_send,
    line_recv,
    cross_send,
    cross_recv,
):
    core, along, across = place()
    answers = greet(core, along, across)
    col = lax.axis_index("col")
    cols = lax.axis_size("col")
    peers = [(col + d) % cols for d in range(1, cols)]
    my_slot = 2 * along + core
    sub = iota((8, B), 0)
    rows = draws_ref.shape[0] * draws_ref.shape[1]
    draws = draws_ref[...].reshape(rows, B)
    held[ZERO_TILE] = jnp.zeros((8, B), F32)

    def to_peers(source, target, which):
        for to in peers:
            remote(source(to), target.at[col], col_send.at[which], col_recv.at[which], {"col": to}).start()

    def from_peers(target, sems, which):
        wait_bytes(target.at[pl.ds(0, cols - 1)], sems.at[which])

    def noise_of(section, tiles_ref):
        tiles = []
        for slot in range(CAP):
            rank = jnp.maximum(rank_ref[CAP * section + slot], 0)
            tile = tiles_ref[rank % cols]
            swapped = pltpu.roll(tile, 4, 0)
            keep = (rank // cols == slot).astype(F32)
            tiles.append(tile * keep + swapped * (1.0 - keep))
        return jnp.where(sub < 4, tiles[0], tiles[1])

    def spread_values(s, tile):
        values[s] = tile
        turned[CAP * s] = tile
        turned[CAP * s + 1] = pltpu.roll(tile, 4, 0)

    def prepare(section, both):
        for slot in range(CAP):
            rank = jnp.maximum(rank_ref[CAP * section + slot], 0)
            place_in_wave = rank % cols
            weight = early[place_in_wave]
            if both:
                is_late = (rank // cols).astype(F32)
                weight = weight * (1.0 - is_late) + late[place_in_wave] * is_late
            part = weight.astype(BF16)
            high[:, slot * B : (slot + 1) * B] = part
            low[:, slot * B : (slot + 1) * B] = (weight - part.astype(F32)).astype(BF16)

    def share(s):
        for device, slot in line_targets(core, along, across):
            remote(
                values.at[s], got_line.at[s, slot], line_send.at[s], line_recv.at[s], {"blk": device}
            ).start()
        got_line[s, my_slot] = values[s]

    def pass_on(s):
        wait_bytes(got_line.at[s, pl.ds(0, 2 * LINE - 1)], line_recv.at[s])
        first = s * (2 * LINE * CAP)
        for dev in range(2 * LINE):
            tile = got_line[s, dev]
            held[first + 2 * dev] = tile
            held[first + 2 * dev + 1] = pltpu.roll(tile, 4, 0)

        def pick(peer, slot_there):
            lanes = (s + 1) * (CAP * K)
            for k in range(K):
                upper = held[key_ref[peer, lanes + k]]
                lower = held[key_ref[peer, lanes + K + k]]
                slot_there[k] = jnp.where(sub < 4, upper, lower)

        for device, peer in cross_peers(core, along, across):
            pick(peer, picked.at[s, peer])
            remote(
                picked.at[s, peer], got_cross.at[s, across], cross_send.at[s], cross_recv.at[s], {"blk": device}
            ).start()
        pick(across, got_cross.at[s, across])

    def collect(s):
        wait_bytes(got_cross.at[s, pl.ds(0, LINE - 1)], cross_recv.at[s])
        near = []
        for k in range(K):
            tiles = [got_cross[s, peer, k] for peer in range(LINE)]
            while len(tiles) > 1:
                tiles = [tiles[i] + tiles[i + 1] for i in range(0, len(tiles), 2)]
            near.append(tiles[0])
        return jnp.concatenate(near, axis=1)

    def update(s, near):
        part = near.astype(BF16).astype(F32)
        both = jnp.concatenate([part, near - part], axis=0).astype(BF16)
        first = jnp.dot(both, high[...], preferred_element_type=F32)
        second = jnp.dot(both[0:8], low[...], preferred_element_type=F32)
        total = first[0:8] + (first[8:16] + second)
        added = jnp.where(sub < 4, total[:, :B], total[:, B:])
        spread_values(s, added + noise_of(s, got_noise))

    build_covariances(slot_ref, there_ref, coords_ref, near_ref, cov)
    own_cov = cov[0, K, :, K * B :]
    first_noise[...] = multiply(draws, panel_factors([own_cov], [False])[0]).reshape(first_noise.shape)
    await_answers(answers)
    to_peers(lambda to: first_noise.at[to], got_first, 0)
    got_first[col] = first_noise[col]

    def after_first():
        from_peers(got_first, col_recv, 0)
        spread_values(0, noise_of(0, got_first))
        share(0)

    def after_second():
        pass_on(0)

    def after_third():
        near_first[...] = collect(0)
        to_peers(lambda to: near_first, got_near, 1)
        got_near[col] = near_first[...]

    def after_fourth():
        pass

    between = (after_first, after_second, after_third, after_fourth)

    def step(k, carry):
        start = pl.multiple_of(k * B, B)
        inverse = panel_factors([cov[q, k, :, pl.ds(start, B)] for q in range(2)], [True, True])
        for q in range(2):
            inverses[q, k] = inverse[q]
        for at in range(K):

            @pl.when(k == at)
            def _(at=at):
                for q in range(2):
                    rest = slice((at + 1) * B, (K + 1) * B)
                    white = multiply(inverse[q], cov[q, at, :, rest])
                    cov[q, at, :, rest] = white
                    for row in range(at + 1, K + 1):
                        first = (row - at - 1) * B
                        cov[q, row, :, row * B :] = cov[q, row, :, row * B :] - multiply_tn(
                            white[:, first : first + B], white[:, first:]
                        )
                between[at]()

        return carry

    lax.fori_loop(0, K, step, 0)
    upper = panel_factors([cov[q, K, :, K * B :] for q in range(2)], [False, False])
    for q in range(2):
        for k in reversed(range(K)):
            total = cov[q, k, :, K * B :]
            if k + 1 < K:
                total = total - multiply(cov[q, k, :, (k + 1) * B : K * B], weights[q, (k + 1) * B :, :])
            weights[q, k * B : (k + 1) * B, :] = multiply_tn(inverses[q, k], total)
    drawn = multiply(draws, jnp.concatenate(upper, axis=1))
    from_peers(got_near, col_recv, 1)
    upper_rows = (iota((rows, K * B), 0) // 4) % 2 == 0
    near = got_near[...].reshape(rows, K * B)
    near_slots = [near, pltpu.roll(near, rows - 4, 0)]
    chosen = jnp.zeros((rows, K * B), F32)
    for slot in range(CAP):
        chosen = chosen + near_slots[slot] * (rank_ref[CAP + slot] == col).astype(F32)
    known = multiply(jnp.where(upper_rows, chosen, 0.0), weights[0])
    mine = jnp.where(upper_rows[:, :B], drawn[:, :B], drawn[:, B:]) + known
    noise[...] = mine.reshape(noise.shape)
    to_peers(lambda to: noise.at[to], got_noise, 2)
    got_noise[col] = noise[col]
    for wave, buffer in ((0, early), (1, late)):
        to_peers(lambda to, wave=wave: weights.at[wave], buffer, 3 + wave)
        pltpu.make_async_copy(weights.at[wave], buffer.at[col], local_sem.at[wave]).start()
    from_peers(got_noise, col_recv, 2)
    spread_values(1, noise_of(1, got_noise))
    share(1)
    pass_on(1)
    from_peers(early, col_recv, 3)
    pltpu.make_async_copy(weights.at[0], early.at[col], local_sem.at[0]).wait()
    from_peers(late, col_recv, 4)
    pltpu.make_async_copy(weights.at[1], late.at[col], local_sem.at[1]).wait()
    prepare(2, True)
    update(2, collect(1))
    share(2)

    def section(s, carry):
        prepare(s + 1, True)
        pass_on(s)
        update(s + 1, collect(s))

        @pl.when(s + 1 < ROUNDS)
        def _():
            share(s + 1)

        return carry

    lax.fori_loop(2, ROUNDS, section, 0)
    for block in range(out_ref.shape[1] // B):
        out_ref[:, block * B : (block + 1) * B] = turned[out_key_ref[block]][0:4]
    from_peers(got_first, col_send, 0)
    from_peers(got_near, col_send, 1)
    from_peers(got_noise, col_send, 2)
    from_peers(early, col_send, 3)
    from_peers(late, col_send, 4)

    def finish(s, carry):
        wait_bytes(got_line.at[s, pl.ds(0, 2 * LINE - 1)], line_send.at[s])
        wait_bytes(got_cross.at[s, pl.ds(0, LINE - 1)], cross_send.at[s])
        return carry

    lax.fori_loop(0, ROUNDS, finish, 0)


VMEM_SPEC = pl.BlockSpec(memory_space=pltpu.VMEM)
SMEM_SPEC = pl.BlockSpec(memory_space=pltpu.SMEM)
VMEM_LIMIT = 40 * 1024 * 1024


def local(coords, neighbours, sections, normals):
    blocks = coords.shape[0]
    cols = lax.axis_size("col")
    col = lax.axis_index("col")
    i32 = jnp.int32
    slots = jnp.arange(blocks, dtype=i32)
    same = sections[None, :] == sections[:, None]
    lower = sections[None, :] < sections[:, None]
    earlier = slots[None, :] < slots[:, None]
    within = jnp.sum((same & earlier).astype(i32), axis=1)
    rank = jnp.sum((lower | (same & earlier)).astype(i32), axis=1)
    by_rank = rank[None, :] == slots[:, None]
    slot_of_rank = jnp.sum(by_rank.astype(i32) * slots[None, :], axis=1)
    cells = jnp.arange(SECTIONS * CAP, dtype=i32)
    in_cell = cells[:, None] == (sections * CAP + within)[None, :]
    rank_of_cell = jnp.sum(in_cell.astype(i32) * (rank + 1)[None, :], axis=1) - 1
    listed = neighbours + 1
    asked = jnp.sum(in_cell.astype(i32)[:, :, None] * listed[None, :, :], axis=1).reshape(-1) - 1
    asked = jnp.pad(asked, (0, B - asked.shape[0]), constant_values=-1)
    mine = jnp.stack([col, col + cols])
    is_mine = rank[None, :] == mine[:, None]
    my_slots = jnp.sum(is_mine.astype(i32) * slots[None, :], axis=1)
    ids = jnp.sum(is_mine.astype(i32)[:, :, None] * listed[None, :, :], axis=1).reshape(-1) - 1
    there = (ids >= 0).astype(i32)
    code = (sections * (2 * LINE * CAP) + within).astype(F32)
    out_key = sections * CAP + within

    def tile(v):
        return jnp.broadcast_to(v[:, None], (blocks, B))

    shape = jax.ShapeDtypeStruct
    near, key, draws = pl.pallas_call(
        exchange_kernel,
        out_shape=(shape((2, 8, B), F32), shape((LINE, B), i32), shape((cols, 8, B), F32)),
        in_specs=[SMEM_SPEC] + [VMEM_SPEC] * 5,
        out_specs=(VMEM_SPEC,) * 3,
        scratch_shapes=[
            pltpu.VMEM((3, 8, B), F32),
            pltpu.VMEM((2, 8, B), i32),
            pltpu.VMEM((cols, 8, B), F32),
            pltpu.VMEM((2 * LINE, 3, 8, B), F32),
            pltpu.VMEM((LINE, 2, 8, B), i32),
            pltpu.VMEM((cols, 8, B), F32),
            pltpu.VMEM((LINE, 2, 8, B), F32),
            pltpu.VMEM((LINE, 2, 8, B), F32),
            pltpu.SemaphoreType.DMA((4,)),
            pltpu.SemaphoreType.DMA((4,)),
        ],
        compiler_params=pltpu.CompilerParams(
            collective_id=0, has_side_effects=True, vmem_limit_bytes=VMEM_LIMIT
        ),
        name="exchange",
    )(slot_of_rank, coords, tile(code), tile(ids), jnp.broadcast_to(asked[None, :], (8, B)), normals)

    return pl.pallas_call(
        sample_kernel,
        out_shape=shape(normals.shape, F32),
        in_specs=[SMEM_SPEC] * 5 + [VMEM_SPEC] * 3,
        out_specs=VMEM_SPEC,
        scratch_shapes=[
            pltpu.VMEM((2, K + 1, B, (K + 1) * B), F32),
            pltpu.VMEM((2, K, B, B), F32),
            pltpu.VMEM((2, K * B, B), F32),
            pltpu.VMEM((cols, 8, B), F32),
            pltpu.VMEM((cols, 8, B), F32),
            pltpu.VMEM((8, K * B), F32),
            pltpu.VMEM((cols, K * B, B), F32),
            pltpu.VMEM((cols, K * B, B), F32),
            pltpu.VMEM((cols, 8, B), F32),
            pltpu.VMEM((cols, 8, B), F32),
            pltpu.VMEM((cols, 8, K * B), F32),
            pltpu.VMEM((SECTIONS, 8, B), F32),
            pltpu.VMEM((SECTIONS * CAP, 8, B), F32),
            pltpu.VMEM((ROUNDS, 2 * LINE, 8, B), F32),
            pltpu.VMEM((ZERO_TILE + 1, 8, B), F32),
            pltpu.VMEM((ROUNDS, LINE, K, 8, B), F32),
            pltpu.VMEM((ROUNDS, LINE, K, 8, B), F32),
            pltpu.VMEM((K * B, CAP * B), BF16),
            pltpu.VMEM((K * B, CAP * B), BF16),
            pltpu.SemaphoreType.DMA((2,)),
            pltpu.SemaphoreType.DMA((5,)),
            pltpu.SemaphoreType.DMA((5,)),
            pltpu.SemaphoreType.DMA((ROUNDS,)),
            pltpu.SemaphoreType.DMA((ROUNDS,)),
            pltpu.SemaphoreType.DMA((ROUNDS,)),
            pltpu.SemaphoreType.DMA((ROUNDS,)),
        ],
        compiler_params=pltpu.CompilerParams(
            collective_id=1, has_side_effects=True, vmem_limit_bytes=VMEM_LIMIT
        ),
        name="sample",
    )(key, rank_of_cell, out_key, my_slots, there, coords, near, draws)


def solution(mesh):
    in_specs = (P("blk", None, None), P("blk", None), P("blk"), P("col", "blk"))
    out_specs = P("col", "blk")
    return jax.shard_map(local, mesh=mesh, in_specs=in_specs, out_specs=out_specs, check_vma=False)
```

```python
import jax
import jax.numpy as jnp
from jax import lax
from jax.experimental import pallas as pl
from jax.experimental.pallas import tpu as pltpu
from jax.sharding import PartitionSpec as P

K = 4
SECTIONS = 8
CAP = 2
B = 128
ROUNDS = SECTIONS - 1
LINE = 8
ZERO_TILE = ROUNDS * 2 * LINE * CAP

length_scale = 0.5
nugget_var = 0.1

HIGHEST = lax.Precision.HIGHEST
F32 = jnp.float32
BF16 = jnp.bfloat16


def iota(shape, dim):
    return lax.broadcasted_iota(jnp.int32, shape, dim)


def place():
    blk = lax.axis_index("blk")
    core = blk % 2
    y = (blk // 2) % LINE
    z = blk // (2 * LINE)
    along = (1 - core) * z + core * y
    across = (1 - core) * y + core * z
    return core, along, across


def device_at(core, along, across, other_core):
    chip = (1 - core) * (along * LINE + across) + core * (across * LINE + along)
    return chip * 2 + other_core


FAR_FIRST = (4, 3, 5, 2, 6, 1, 7)


def line_targets(core, along, across):
    targets = []
    for d in FAR_FIRST + (0,):
        if d:
            targets.append((device_at(core, (along + d) % LINE, across, core), 2 * along + core))
        targets.append((device_at(core, along, (across + d) % LINE, 1 - core), 2 * across + core))
    return targets


def line_sources(core, along, across):
    same = [device_at(core, (along + d) % LINE, across, core) for d in range(1, LINE)]
    other = [device_at(core, (along + d) % LINE, across, 1 - core) for d in range(LINE)]
    return same + other


def cross_peers(core, along, across):
    return [
        (device_at(core, along, (across + d) % LINE, core), (across + d) % LINE) for d in FAR_FIRST
    ]


def greet(core, along, across):
    barrier = pltpu.get_barrier_semaphore()
    col = lax.axis_index("col")
    cols = lax.axis_size("col")
    mesh_id = pl.DeviceIdType.MESH
    sources = line_sources(core, along, across) + [device for device, _ in cross_peers(core, along, across)]
    for device in sources:
        pl.semaphore_signal(barrier, inc=1, device_id={"blk": device}, device_id_type=mesh_id)
    for d in range(1, cols):
        pl.semaphore_signal(barrier, inc=1, device_id={"col": (col + d) % cols}, device_id_type=mesh_id)
    return len(sources) + cols - 1


def await_answers(count):
    pl.semaphore_wait(pltpu.get_barrier_semaphore(), count)


def remote(src, dst, send_sem, recv_sem, device_id):
    return pltpu.make_async_remote_copy(
        src_ref=src,
        dst_ref=dst,
        send_sem=send_sem,
        recv_sem=recv_sem,
        device_id=device_id,
        device_id_type=pl.DeviceIdType.MESH,
    )


def wait_bytes(ref, sem):
    pltpu.make_async_copy(ref, ref, sem).wait()


def exchange_kernel(
    slot_ref,
    coords_ref,
    code_ref,
    ids_ref,
    asked_ref,
    normals_ref,
    near_ref,
    key_ref,
    draws_ref,
    own_a,
    own_b,
    own_n,
    got_a,
    got_b,
    got_n,
    picked,
    got_p,
    send_sems,
    recv_sems,
):
    core, along, across = place()
    answers = greet(core, along, across)
    col = lax.axis_index("col")
    cols = lax.axis_size("col")
    my_slot = 2 * along + core
    own_a[0] = coords_ref[:, 0, :]
    own_a[1] = coords_ref[:, 1, :]
    own_a[2] = code_ref[...]
    own_b[0] = ids_ref[...]
    own_b[1] = asked_ref[...]
    for owner in range(cols):
        for half in range(2):
            slot = slot_ref[owner + half * cols]
            drawn = jnp.zeros((4, B), F32)
            for at in range(LINE):
                drawn = drawn + normals_ref[:, at * B : (at + 1) * B] * (slot == at).astype(F32)
            own_n[owner, half * 4 : half * 4 + 4, :] = drawn
    await_answers(answers)
    for device, slot in line_targets(core, along, across):
        remote(own_a, got_a.at[slot], send_sems.at[0], recv_sems.at[0], {"blk": device}).start()
    for device, _ in cross_peers(core, along, across):
        remote(own_b, got_b.at[across], send_sems.at[1], recv_sems.at[1], {"blk": device}).start()
    for d in range(1, cols):
        to = (col + d) % cols
        remote(own_n.at[to], got_n.at[col], send_sems.at[2], recv_sems.at[2], {"col": to}).start()
    got_a[my_slot] = own_a[...]
    got_b[across] = own_b[...]
    got_n[col] = own_n[col]
    lane = iota((1, B), 1)
    lane_dev = device_at(core, lane // (2 * LINE), across, (lane // LINE) % 2)
    lane_block = lane_dev * LINE + lane % LINE
    sub = iota((LINE, B), 0)
    entry_half = (iota((1, B), 1) // K) % 2
    wait_bytes(got_a.at[pl.ds(0, 2 * LINE - 1)], recv_sems.at[0])
    wait_bytes(got_b.at[pl.ds(0, LINE - 1)], recv_sems.at[1])
    chosen = jnp.concatenate(
        [(got_b[peer, 0] == lane_block).astype(F32) for peer in range(LINE)], axis=0
    )
    for axis in range(2):
        held = got_a[:, axis].reshape(B, B)
        moved = jnp.dot(chosen, held, precision=HIGHEST, preferred_element_type=F32)
        picked[:, axis] = moved.reshape(LINE, LINE, B)
    for device, peer in cross_peers(core, along, across):
        remote(picked.at[peer], got_p.at[across], send_sems.at[3], recv_sems.at[3], {"blk": device}).start()
    got_p[across] = picked[across]
    sums = [jnp.zeros((LINE, B), jnp.int32) for _ in range(LINE)]
    for dev in range(2 * LINE):
        block = device_at(core, dev // 2, across, dev % 2) * LINE + sub
        value = got_a[dev, 2].astype(jnp.int32) + (2 * dev + 1)
        for peer in range(LINE):
            sums[peer] = sums[peer] + jnp.where(block == got_b[peer, 1], value, 0)
    for peer in range(LINE):
        total = jnp.sum(sums[peer], axis=0, keepdims=True)
        value = total - 1
        turned = value + entry_half * (1 - 2 * (value % 2))
        key_ref[peer : peer + 1, :] = jnp.where(total > 0, turned, ZERO_TILE)
    wait_bytes(got_n.at[pl.ds(0, cols - 1)], recv_sems.at[2])
    draws_ref[...] = got_n[...]
    wait_bytes(got_p.at[pl.ds(0, LINE - 1)], recv_sems.at[3])
    for axis in range(2):
        near = got_p[0, axis]
        for peer in range(1, LINE):
            near = near + got_p[peer, axis]
        near_ref[axis] = near
    wait_bytes(got_a.at[pl.ds(0, 2 * LINE - 1)], send_sems.at[0])
    wait_bytes(got_b.at[pl.ds(0, LINE - 1)], send_sems.at[1])
    wait_bytes(got_n.at[pl.ds(0, cols - 1)], send_sems.at[2])
    wait_bytes(got_p.at[pl.ds(0, LINE - 1)], send_sems.at[3])


def split3(x):
    high = x.astype(BF16).astype(F32)
    rest = x - high
    middle = rest.astype(BF16).astype(F32)
    return high, middle, rest - middle


def thin_product(left, right):
    l1, l2, l3 = split3(left)
    r1, r2, r3 = split3(right)
    tall_left = jnp.concatenate([l1, l1, l2, l2, l1, l3], axis=0).astype(BF16)
    tall_right = jnp.concatenate([r1, r2, r1, r2, r3, r1], axis=0).astype(BF16)
    return lax.dot_general(tall_left, tall_right, (((0,), (0,)), ((), ())), preferred_element_type=F32)


def spread(tile, first):
    return [jnp.take_along_axis(tile, jnp.full((8, B), first + j, jnp.int32), axis=1) for j in range(8)]


def weighted_rows(factors, rows):
    terms = [factors[j] * rows[j : j + 1, :] for j in range(8)]
    return ((terms[0] + terms[1]) + (terms[2] + terms[3])) + ((terms[4] + terms[5]) + (terms[6] + terms[7]))


def eliminate(rows, columns, sub):
    columns = list(columns)
    full = rows
    scales = []
    for j in range(8):
        below, here = sub > j, sub == j
        pivot = columns[j][j : j + 1, :]
        inverse = 1.0 / pivot
        factors = columns[j] * inverse
        under = jnp.where(below, factors, 0.0)
        scaled = full[j : j + 1, :] * inverse
        full = jnp.where(here, scaled, full - columns[j] * scaled)
        rows = rows - under * rows[j : j + 1, :]
        for later in range(j + 1, 8):
            columns[later] = jnp.where(
                here, columns[later] * inverse, columns[later] - factors * columns[later][j : j + 1, :]
            )
        scales.append(lax.rsqrt(pivot))
    scale = scales[7]
    for j in range(7):
        scale = jnp.where(sub == j, scales[j], scale)
    return rows * scale, full


def panel_factors(matrices, inverted):
    sub, lane = iota((8, B), 0), iota((8, B), 1)
    wide = iota((B, B), 1)
    matrices = list(matrices)
    ahead = [m[0:8] for m in matrices]
    panels = [[] for _ in matrices]
    for panel in range(B // 8):
        at = 8 * panel
        inside = (lane >= at) & (lane < at + 8)
        for q in range(len(matrices)):
            rows, left = ahead[q], matrices[q]
            if inverted[q]:
                unit = jnp.where(lane == sub + at, 1.0, 0.0)
                done, full = eliminate(jnp.where(inside, unit, rows), spread(rows, at), sub)
                panels[q].append(jnp.where(lane < at + 8, done, 0.0))
            else:
                done, full = eliminate(rows, spread(rows, at), sub)
                panels[q].append(jnp.where(lane >= sub + at, done, 0.0))
            if at + 8 < B:
                following = left[at + 8 : at + 16]
                drop = weighted_rows(spread(following, at), full)
                if inverted[q]:
                    following = jnp.where(inside, 0.0, following)
                    left = jnp.where((wide >= at) & (wide < at + 8), 0.0, left)
                ahead[q] = following - drop
                matrices[q] = left - thin_product(done, done)
    return [jnp.concatenate(p, axis=0) for p in panels]


def multiply(left, right):
    return jnp.dot(left, right, precision=HIGHEST, preferred_element_type=F32)


def multiply_tn(left, right):
    return lax.dot_general(
        left, right, (((0,), (0,)), ((), ())), precision=HIGHEST, preferred_element_type=F32
    )


def covariance(row_x, row_y, col_x, col_y):
    dx = col_x - row_x
    dy = col_y - row_y
    return jnp.exp(-jnp.sqrt(dx * dx + dy * dy) / length_scale)


def build_covariances(slot_ref, there_ref, coords_ref, near_ref, cov):
    eye = (iota((B, B), 0) == iota((B, B), 1)).astype(F32)
    for q in range(2):
        own = coords_ref[slot_ref[q]]
        points = [
            (near_ref[0, q * K + k : q * K + k + 1, :], near_ref[1, q * K + k : q * K + k + 1, :])
            for k in range(K)
        ] + [(own[0:1], own[1:2])]
        there = [there_ref[q * K + k].astype(F32) for k in range(K)] + [jnp.float32(1.0)]
        for a in range(K + 1):
            col_x = jnp.broadcast_to(points[a][0], (B, B)).T
            col_y = jnp.broadcast_to(points[a][1], (B, B)).T
            for b in range(a, K + 1):
                block = covariance(points[b][0], points[b][1], col_x, col_y) * (there[a] * there[b])
                if a == b:
                    block = block + (nugget_var * there[a] + (1.0 - there[a])) * eye
                cov[q, a, :, b * B : (b + 1) * B] = block


def sample_kernel(
    key_ref,
    rank_ref,
    out_key_ref,
    slot_ref,
    there_ref,
    coords_ref,
    near_ref,
    draws_ref,
    out_ref,
    cov,
    inverses,
    weights,
    first_cov,
    first_noise,
    noise,
    near_first,
    early,
    late,
    got_first,
    got_noise,
    got_near,
    values,
    turned,
    got_line,
    held,
    picked,
    got_cross,
    high,
    low,
    local_sem,
    col_send,
    col_recv,
    line_send,
    line_recv,
    cross_send,
    cross_recv,
):
    core, along, across = place()
    answers = greet(core, along, across)
    col = lax.axis_index("col")
    cols = lax.axis_size("col")
    peers = [(col + d) % cols for d in range(1, cols)]
    my_slot = 2 * along + core
    sub = iota((8, B), 0)
    rows = draws_ref.shape[0] * draws_ref.shape[1]
    draws = draws_ref[...].reshape(rows, B)
    held[ZERO_TILE] = jnp.zeros((8, B), F32)

    def to_peers(source, target, which):
        for to in peers:
            remote(source(to), target.at[col], col_send.at[which], col_recv.at[which], {"col": to}).start()

    def from_peers(target, sems, which):
        wait_bytes(target.at[pl.ds(0, cols - 1)], sems.at[which])

    def noise_of(section, tiles_ref):
        tiles = []
        for slot in range(CAP):
            rank = jnp.maximum(rank_ref[CAP * section + slot], 0)
            tile = tiles_ref[rank % cols]
            swapped = pltpu.roll(tile, 4, 0)
            keep = (rank // cols == slot).astype(F32)
            tiles.append(tile * keep + swapped * (1.0 - keep))
        return jnp.where(sub < 4, tiles[0], tiles[1])

    def spread_values(s, tile):
        values[s] = tile
        turned[CAP * s] = tile
        turned[CAP * s + 1] = pltpu.roll(tile, 4, 0)

    def prepare(section, both):
        for slot in range(CAP):
            rank = jnp.maximum(rank_ref[CAP * section + slot], 0)
            place_in_wave = rank % cols
            weight = early[place_in_wave]
            if both:
                is_late = (rank // cols).astype(F32)
                weight = weight * (1.0 - is_late) + late[place_in_wave] * is_late
            part = weight.astype(BF16)
            high[:, slot * B : (slot + 1) * B] = part
            low[:, slot * B : (slot + 1) * B] = (weight - part.astype(F32)).astype(BF16)

    def share(s):
        for device, slot in line_targets(core, along, across):
            remote(
                values.at[s], got_line.at[s, slot], line_send.at[s], line_recv.at[s], {"blk": device}
            ).start()
        got_line[s, my_slot] = values[s]

    def pass_on(s):
        wait_bytes(got_line.at[s, pl.ds(0, 2 * LINE - 1)], line_recv.at[s])
        first = s * (2 * LINE * CAP)
        for dev in range(2 * LINE):
            tile = got_line[s, dev]
            held[first + 2 * dev] = tile
            held[first + 2 * dev + 1] = pltpu.roll(tile, 4, 0)

        def pick(peer, slot_there):
            lanes = (s + 1) * (CAP * K)
            for k in range(K):
                upper = held[key_ref[peer, lanes + k]]
                lower = held[key_ref[peer, lanes + K + k]]
                slot_there[k] = jnp.where(sub < 4, upper, lower)

        for device, peer in cross_peers(core, along, across):
            pick(peer, picked.at[s, peer])
            remote(
                picked.at[s, peer], got_cross.at[s, across], cross_send.at[s], cross_recv.at[s], {"blk": device}
            ).start()
        pick(across, got_cross.at[s, across])

    def collect(s):
        wait_bytes(got_cross.at[s, pl.ds(0, LINE - 1)], cross_recv.at[s])
        near = []
        for k in range(K):
            tiles = [got_cross[s, peer, k] for peer in range(LINE)]
            while len(tiles) > 1:
                tiles = [tiles[i] + tiles[i + 1] for i in range(0, len(tiles), 2)]
            near.append(tiles[0])
        return jnp.concatenate(near, axis=1)

    def update(s, near):
        part = near.astype(BF16).astype(F32)
        both = jnp.concatenate([part, near - part], axis=0).astype(BF16)
        first = jnp.dot(both, high[...], preferred_element_type=F32)
        second = jnp.dot(both[0:8], low[...], preferred_element_type=F32)
        total = first[0:8] + (first[8:16] + second)
        added = jnp.where(sub < 4, total[:, :B], total[:, B:])
        spread_values(s, added + noise_of(s, got_noise))

    build_covariances(slot_ref, there_ref, coords_ref, near_ref, cov)
    first_cov[...] = cov[0, K, :, K * B :]

    def after_first(first_upper):
        first_noise[...] = multiply(draws, first_upper).reshape(first_noise.shape)
        await_answers(answers)
        to_peers(lambda to: first_noise.at[to], got_first, 0)
        got_first[col] = first_noise[col]

    def after_second(_):
        from_peers(got_first, col_recv, 0)
        spread_values(0, noise_of(0, got_first))
        share(0)

    def after_third(_):
        pass_on(0)

    def after_fourth(_):
        near_first[...] = collect(0)
        to_peers(lambda to: near_first, got_near, 1)
        got_near[col] = near_first[...]

    between = (after_first, after_second, after_third, after_fourth)

    def step(k, carry):
        start = pl.multiple_of(k * B, B)
        matrices = [cov[q, k, :, pl.ds(start, B)] for q in range(2)] + [first_cov[...]]
        *inverse, first_upper = panel_factors(matrices, [True, True, False])
        for q in range(2):
            inverses[q, k] = inverse[q]
        for at in range(K):

            @pl.when(k == at)
            def _(at=at):
                for q in range(2):
                    rest = slice((at + 1) * B, (K + 1) * B)
                    white = multiply(inverse[q], cov[q, at, :, rest])
                    cov[q, at, :, rest] = white
                    for row in range(at + 1, K + 1):
                        first = (row - at - 1) * B
                        cov[q, row, :, row * B :] = cov[q, row, :, row * B :] - multiply_tn(
                            white[:, first : first + B], white[:, first:]
                        )
                between[at](first_upper)

        return carry

    lax.fori_loop(0, K, step, 0)
    upper = panel_factors([cov[q, K, :, K * B :] for q in range(2)], [False, False])
    for q in range(2):
        for k in reversed(range(K)):
            total = cov[q, k, :, K * B :]
            if k + 1 < K:
                total = total - multiply(cov[q, k, :, (k + 1) * B : K * B], weights[q, (k + 1) * B :, :])
            weights[q, k * B : (k + 1) * B, :] = multiply_tn(inverses[q, k], total)
    drawn = multiply(draws, jnp.concatenate(upper, axis=1))
    from_peers(got_near, col_recv, 1)
    upper_rows = (iota((rows, K * B), 0) // 4) % 2 == 0
    near = got_near[...].reshape(rows, K * B)
    near_slots = [near, pltpu.roll(near, rows - 4, 0)]
    chosen = jnp.zeros((rows, K * B), F32)
    for slot in range(CAP):
        chosen = chosen + near_slots[slot] * (rank_ref[CAP + slot] == col).astype(F32)
    known = multiply(jnp.where(upper_rows, chosen, 0.0), weights[0])
    mine = jnp.where(upper_rows[:, :B], drawn[:, :B], drawn[:, B:]) + known
    noise[...] = mine.reshape(noise.shape)
    to_peers(lambda to: noise.at[to], got_noise, 2)
    got_noise[col] = noise[col]
    for wave, buffer in ((0, early), (1, late)):
        to_peers(lambda to, wave=wave: weights.at[wave], buffer, 3 + wave)
        pltpu.make_async_copy(weights.at[wave], buffer.at[col], local_sem.at[wave]).start()
    from_peers(got_noise, col_recv, 2)
    spread_values(1, noise_of(1, got_noise))
    share(1)
    pass_on(1)
    from_peers(early, col_recv, 3)
    pltpu.make_async_copy(weights.at[0], early.at[col], local_sem.at[0]).wait()
    prepare(2, False)
    update(2, collect(1))
    share(2)
    from_peers(late, col_recv, 4)
    pltpu.make_async_copy(weights.at[1], late.at[col], local_sem.at[1]).wait()

    def section(s, carry):
        prepare(s + 1, True)
        pass_on(s)
        update(s + 1, collect(s))

        @pl.when(s + 1 < ROUNDS)
        def _():
            share(s + 1)

        return carry

    lax.fori_loop(2, ROUNDS, section, 0)
    for block in range(out_ref.shape[1] // B):
        out_ref[:, block * B : (block + 1) * B] = turned[out_key_ref[block]][0:4]
    from_peers(got_first, col_send, 0)
    from_peers(got_near, col_send, 1)
    from_peers(got_noise, col_send, 2)
    from_peers(early, col_send, 3)
    from_peers(late, col_send, 4)

    def finish(s, carry):
        wait_bytes(got_line.at[s, pl.ds(0, 2 * LINE - 1)], line_send.at[s])
        wait_bytes(got_cross.at[s, pl.ds(0, LINE - 1)], cross_send.at[s])
        return carry

    lax.fori_loop(0, ROUNDS, finish, 0)


VMEM_SPEC = pl.BlockSpec(memory_space=pltpu.VMEM)
SMEM_SPEC = pl.BlockSpec(memory_space=pltpu.SMEM)
VMEM_LIMIT = 40 * 1024 * 1024


def local(coords, neighbours, sections, normals):
    blocks = coords.shape[0]
    cols = lax.axis_size("col")
    col = lax.axis_index("col")
    i32 = jnp.int32
    slots = jnp.arange(blocks, dtype=i32)
    same = sections[None, :] == sections[:, None]
    lower = sections[None, :] < sections[:, None]
    earlier = slots[None, :] < slots[:, None]
    within = jnp.sum((same & earlier).astype(i32), axis=1)
    rank = jnp.sum((lower | (same & earlier)).astype(i32), axis=1)
    by_rank = rank[None, :] == slots[:, None]
    slot_of_rank = jnp.sum(by_rank.astype(i32) * slots[None, :], axis=1)
    cells = jnp.arange(SECTIONS * CAP, dtype=i32)
    in_cell = cells[:, None] == (sections * CAP + within)[None, :]
    rank_of_cell = jnp.sum(in_cell.astype(i32) * (rank + 1)[None, :], axis=1) - 1
    listed = neighbours + 1
    asked = jnp.sum(in_cell.astype(i32)[:, :, None] * listed[None, :, :], axis=1).reshape(-1) - 1
    asked = jnp.pad(asked, (0, B - asked.shape[0]), constant_values=-1)
    mine = jnp.stack([col, col + cols])
    is_mine = rank[None, :] == mine[:, None]
    my_slots = jnp.sum(is_mine.astype(i32) * slots[None, :], axis=1)
    ids = jnp.sum(is_mine.astype(i32)[:, :, None] * listed[None, :, :], axis=1).reshape(-1) - 1
    there = (ids >= 0).astype(i32)
    code = (sections * (2 * LINE * CAP) + within).astype(F32)
    out_key = sections * CAP + within

    def tile(v):
        return jnp.broadcast_to(v[:, None], (blocks, B))

    shape = jax.ShapeDtypeStruct
    near, key, draws = pl.pallas_call(
        exchange_kernel,
        out_shape=(shape((2, 8, B), F32), shape((LINE, B), i32), shape((cols, 8, B), F32)),
        in_specs=[SMEM_SPEC] + [VMEM_SPEC] * 5,
        out_specs=(VMEM_SPEC,) * 3,
        scratch_shapes=[
            pltpu.VMEM((3, 8, B), F32),
            pltpu.VMEM((2, 8, B), i32),
            pltpu.VMEM((cols, 8, B), F32),
            pltpu.VMEM((2 * LINE, 3, 8, B), F32),
            pltpu.VMEM((LINE, 2, 8, B), i32),
            pltpu.VMEM((cols, 8, B), F32),
            pltpu.VMEM((LINE, 2, 8, B), F32),
            pltpu.VMEM((LINE, 2, 8, B), F32),
            pltpu.SemaphoreType.DMA((4,)),
            pltpu.SemaphoreType.DMA((4,)),
        ],
        compiler_params=pltpu.CompilerParams(
            collective_id=0, has_side_effects=True, vmem_limit_bytes=VMEM_LIMIT
        ),
        name="exchange",
    )(slot_of_rank, coords, tile(code), tile(ids), jnp.broadcast_to(asked[None, :], (8, B)), normals)

    return pl.pallas_call(
        sample_kernel,
        out_shape=shape(normals.shape, F32),
        in_specs=[SMEM_SPEC] * 5 + [VMEM_SPEC] * 3,
        out_specs=VMEM_SPEC,
        scratch_shapes=[
            pltpu.VMEM((2, K + 1, B, (K + 1) * B), F32),
            pltpu.VMEM((2, K, B, B), F32),
            pltpu.VMEM((2, K * B, B), F32),
            pltpu.VMEM((B, B), F32),
            pltpu.VMEM((cols, 8, B), F32),
            pltpu.VMEM((cols, 8, B), F32),
            pltpu.VMEM((8, K * B), F32),
            pltpu.VMEM((cols, K * B, B), F32),
            pltpu.VMEM((cols, K * B, B), F32),
            pltpu.VMEM((cols, 8, B), F32),
            pltpu.VMEM((cols, 8, B), F32),
            pltpu.VMEM((cols, 8, K * B), F32),
            pltpu.VMEM((SECTIONS, 8, B), F32),
            pltpu.VMEM((SECTIONS * CAP, 8, B), F32),
            pltpu.VMEM((ROUNDS, 2 * LINE, 8, B), F32),
            pltpu.VMEM((ZERO_TILE + 1, 8, B), F32),
            pltpu.VMEM((ROUNDS, LINE, K, 8, B), F32),
            pltpu.VMEM((ROUNDS, LINE, K, 8, B), F32),
            pltpu.VMEM((K * B, CAP * B), BF16),
            pltpu.VMEM((K * B, CAP * B), BF16),
            pltpu.SemaphoreType.DMA((2,)),
            pltpu.SemaphoreType.DMA((5,)),
            pltpu.SemaphoreType.DMA((5,)),
            pltpu.SemaphoreType.DMA((ROUNDS,)),
            pltpu.SemaphoreType.DMA((ROUNDS,)),
            pltpu.SemaphoreType.DMA((ROUNDS,)),
            pltpu.SemaphoreType.DMA((ROUNDS,)),
        ],
        compiler_params=pltpu.CompilerParams(
            collective_id=1, has_side_effects=True, vmem_limit_bytes=VMEM_LIMIT
        ),
        name="sample",
    )(key, rank_of_cell, out_key, my_slots, there, coords, near, draws)


def solution(mesh):
    in_specs = (P("blk", None, None), P("blk", None), P("blk"), P("col", "blk"))
    out_specs = P("col", "blk")
    return jax.shard_map(local, mesh=mesh, in_specs=in_specs, out_specs=out_specs, check_vma=False)
```

```python
import jax
import jax.numpy as jnp
from jax import lax
from jax.experimental import pallas as pl
from jax.experimental.pallas import tpu as pltpu
from jax.sharding import PartitionSpec as P

K = 4
SECTIONS = 8
CAP = 2
B = 128
ROUNDS = SECTIONS - 1
LINE = 8
ZERO_TILE = ROUNDS * 2 * LINE * CAP

length_scale = 0.5
nugget_var = 0.1

HIGHEST = lax.Precision.HIGHEST
F32 = jnp.float32
BF16 = jnp.bfloat16


def iota(shape, dim):
    return lax.broadcasted_iota(jnp.int32, shape, dim)


def place():
    blk = lax.axis_index("blk")
    core = blk % 2
    y = (blk // 2) % LINE
    z = blk // (2 * LINE)
    along = (1 - core) * z + core * y
    across = (1 - core) * y + core * z
    return core, along, across


def device_at(core, along, across, other_core):
    chip = (1 - core) * (along * LINE + across) + core * (across * LINE + along)
    return chip * 2 + other_core


FAR_FIRST = (4, 3, 5, 2, 6, 1, 7)


def line_targets(core, along, across):
    targets = []
    for d in FAR_FIRST + (0,):
        if d:
            targets.append((device_at(core, (along + d) % LINE, across, core), 2 * along + core))
        targets.append((device_at(core, along, (across + d) % LINE, 1 - core), 2 * across + core))
    return targets


def line_sources(core, along, across):
    same = [device_at(core, (along + d) % LINE, across, core) for d in range(1, LINE)]
    other = [device_at(core, (along + d) % LINE, across, 1 - core) for d in range(LINE)]
    return same + other


def cross_peers(core, along, across):
    return [
        (device_at(core, along, (across + d) % LINE, core), (across + d) % LINE) for d in FAR_FIRST
    ]


def greet(core, along, across):
    barrier = pltpu.get_barrier_semaphore()
    col = lax.axis_index("col")
    cols = lax.axis_size("col")
    mesh_id = pl.DeviceIdType.MESH
    sources = line_sources(core, along, across) + [device for device, _ in cross_peers(core, along, across)]
    for device in sources:
        pl.semaphore_signal(barrier, inc=1, device_id={"blk": device}, device_id_type=mesh_id)
    for d in range(1, cols):
        pl.semaphore_signal(barrier, inc=1, device_id={"col": (col + d) % cols}, device_id_type=mesh_id)
    return len(sources) + cols - 1


def await_answers(count):
    pl.semaphore_wait(pltpu.get_barrier_semaphore(), count)


def remote(src, dst, send_sem, recv_sem, device_id):
    return pltpu.make_async_remote_copy(
        src_ref=src,
        dst_ref=dst,
        send_sem=send_sem,
        recv_sem=recv_sem,
        device_id=device_id,
        device_id_type=pl.DeviceIdType.MESH,
    )


def wait_bytes(ref, sem):
    pltpu.make_async_copy(ref, ref, sem).wait()


def exchange_kernel(
    sections_ref,
    neighbours_ref,
    coords_ref,
    normals_ref,
    near_ref,
    key_ref,
    draws_ref,
    rank_ref,
    out_key_ref,
    slot_ref,
    there_ref,
    own_a,
    own_b,
    own_n,
    got_a,
    got_b,
    got_n,
    picked,
    got_p,
    send_sems,
    recv_sems,
):
    core, along, across = place()
    answers = greet(core, along, across)
    col = lax.axis_index("col")
    cols = lax.axis_size("col")
    my_slot = 2 * along + core
    sub, lane = iota((8, B), 0), iota((8, B), 1)
    blocks = range(LINE)

    def flag(condition):
        return condition.astype(jnp.int32)

    section = [sections_ref[i] for i in blocks]
    listed = [[neighbours_ref[i, k] for k in range(K)] for i in blocks]
    within = [sum((flag(section[j] == section[i]) for j in range(i)), jnp.int32(0)) for i in blocks]
    rank = [within[i] + sum(flag(section[j] < section[i]) for j in blocks) for i in blocks]
    cell = [section[i] * CAP + within[i] for i in blocks]
    for c in range(SECTIONS * CAP):
        rank_ref[c] = sum(flag(cell[i] == c) * (rank[i] + 1) for i in blocks) - 1
    code = jnp.zeros((8, B), F32)
    asked = jnp.full((8, B), -1, jnp.int32)
    for i in blocks:
        out_key_ref[i] = cell[i]
        code = jnp.where(sub == i, (section[i] * (2 * LINE * CAP) + within[i]).astype(F32), code)
        for k in range(K):
            asked = jnp.where(lane == cell[i] * K + k, listed[i][k], asked)
    ids = jnp.full((8, B), -1, jnp.int32)
    for half in range(2):
        mine = [flag(rank[i] == col + half * cols) for i in blocks]
        slot_ref[half] = sum(mine[i] * i for i in blocks)
        for k in range(K):
            entry = sum(mine[i] * (listed[i][k] + 1) for i in blocks) - 1
            there_ref[half * K + k] = flag(entry >= 0)
            ids = jnp.where(sub == half * K + k, entry, ids)
    own_a[0] = coords_ref[:, 0, :]
    own_a[1] = coords_ref[:, 1, :]
    own_a[2] = code
    own_b[0] = ids
    own_b[1] = asked
    for owner in range(cols):
        for half in range(2):
            drawn = jnp.zeros((4, B), F32)
            for i in blocks:
                chosen = (rank[i] == owner + half * cols).astype(F32)
                drawn = drawn + normals_ref[:, i * B : (i + 1) * B] * chosen
            own_n[owner, half * 4 : half * 4 + 4, :] = drawn
    await_answers(answers)
    for device, slot in line_targets(core, along, across):
        remote(own_a, got_a.at[slot], send_sems.at[0], recv_sems.at[0], {"blk": device}).start()
    for device, _ in cross_peers(core, along, across):
        remote(own_b, got_b.at[across], send_sems.at[1], recv_sems.at[1], {"blk": device}).start()
    for d in range(1, cols):
        to = (col + d) % cols
        remote(own_n.at[to], got_n.at[col], send_sems.at[2], recv_sems.at[2], {"col": to}).start()
    got_a[my_slot] = own_a[...]
    got_b[across] = own_b[...]
    got_n[col] = own_n[col]
    lane = iota((1, B), 1)
    lane_dev = device_at(core, lane // (2 * LINE), across, (lane // LINE) % 2)
    lane_block = lane_dev * LINE + lane % LINE
    sub = iota((LINE, B), 0)
    entry_half = (iota((1, B), 1) // K) % 2
    wait_bytes(got_a.at[pl.ds(0, 2 * LINE - 1)], recv_sems.at[0])
    wait_bytes(got_b.at[pl.ds(0, LINE - 1)], recv_sems.at[1])
    chosen = jnp.concatenate(
        [(got_b[peer, 0] == lane_block).astype(F32) for peer in range(LINE)], axis=0
    )
    for axis in range(2):
        held = got_a[:, axis].reshape(B, B)
        moved = jnp.dot(chosen, held, precision=HIGHEST, preferred_element_type=F32)
        picked[:, axis] = moved.reshape(LINE, LINE, B)
    for device, peer in cross_peers(core, along, across):
        remote(picked.at[peer], got_p.at[across], send_sems.at[3], recv_sems.at[3], {"blk": device}).start()
    got_p[across] = picked[across]
    sums = [jnp.zeros((LINE, B), jnp.int32) for _ in range(LINE)]
    for dev in range(2 * LINE):
        block = device_at(core, dev // 2, across, dev % 2) * LINE + sub
        value = got_a[dev, 2].astype(jnp.int32) + (2 * dev + 1)
        for peer in range(LINE):
            sums[peer] = sums[peer] + jnp.where(block == got_b[peer, 1], value, 0)
    for peer in range(LINE):
        total = jnp.sum(sums[peer], axis=0, keepdims=True)
        value = total - 1
        turned = value + entry_half * (1 - 2 * (value % 2))
        key_ref[peer : peer + 1, :] = jnp.where(total > 0, turned, ZERO_TILE)
    wait_bytes(got_n.at[pl.ds(0, cols - 1)], recv_sems.at[2])
    draws_ref[...] = got_n[...]
    wait_bytes(got_p.at[pl.ds(0, LINE - 1)], recv_sems.at[3])
    for axis in range(2):
        near = got_p[0, axis]
        for peer in range(1, LINE):
            near = near + got_p[peer, axis]
        near_ref[axis] = near
    wait_bytes(got_a.at[pl.ds(0, 2 * LINE - 1)], send_sems.at[0])
    wait_bytes(got_b.at[pl.ds(0, LINE - 1)], send_sems.at[1])
    wait_bytes(got_n.at[pl.ds(0, cols - 1)], send_sems.at[2])
    wait_bytes(got_p.at[pl.ds(0, LINE - 1)], send_sems.at[3])


def split3(x):
    high = x.astype(BF16).astype(F32)
    rest = x - high
    middle = rest.astype(BF16).astype(F32)
    return high, middle, rest - middle


def thin_product(left, right):
    l1, l2, l3 = split3(left)
    r1, r2, r3 = split3(right)
    tall_left = jnp.concatenate([l1, l1, l2, l2, l1, l3], axis=0).astype(BF16)
    tall_right = jnp.concatenate([r1, r2, r1, r2, r3, r1], axis=0).astype(BF16)
    return lax.dot_general(tall_left, tall_right, (((0,), (0,)), ((), ())), preferred_element_type=F32)


def spread(tile, first):
    return [jnp.take_along_axis(tile, jnp.full((8, B), first + j, jnp.int32), axis=1) for j in range(8)]


def weighted_rows(factors, rows):
    terms = [factors[j] * rows[j : j + 1, :] for j in range(8)]
    return ((terms[0] + terms[1]) + (terms[2] + terms[3])) + ((terms[4] + terms[5]) + (terms[6] + terms[7]))


def eliminate(rows, columns, sub):
    columns = list(columns)
    full = rows
    scales = []
    for j in range(8):
        below, here = sub > j, sub == j
        pivot = columns[j][j : j + 1, :]
        inverse = 1.0 / pivot
        factors = columns[j] * inverse
        under = jnp.where(below, factors, 0.0)
        scaled = full[j : j + 1, :] * inverse
        full = jnp.where(here, scaled, full - columns[j] * scaled)
        rows = rows - under * rows[j : j + 1, :]
        for later in range(j + 1, 8):
            columns[later] = jnp.where(
                here, columns[later] * inverse, columns[later] - factors * columns[later][j : j + 1, :]
            )
        scales.append(lax.rsqrt(pivot))
    scale = scales[7]
    for j in range(7):
        scale = jnp.where(sub == j, scales[j], scale)
    return rows * scale, full


def panel_factors(matrices, inverted):
    sub, lane = iota((8, B), 0), iota((8, B), 1)
    wide = iota((B, B), 1)
    matrices = list(matrices)
    ahead = [m[0:8] for m in matrices]
    panels = [[] for _ in matrices]
    for panel in range(B // 8):
        at = 8 * panel
        inside = (lane >= at) & (lane < at + 8)
        for q in range(len(matrices)):
            rows, left = ahead[q], matrices[q]
            if inverted[q]:
                unit = jnp.where(lane == sub + at, 1.0, 0.0)
                done, full = eliminate(jnp.where(inside, unit, rows), spread(rows, at), sub)
                panels[q].append(jnp.where(lane < at + 8, done, 0.0))
            else:
                done, full = eliminate(rows, spread(rows, at), sub)
                panels[q].append(jnp.where(lane >= sub + at, done, 0.0))
            if at + 8 < B:
                following = left[at + 8 : at + 16]
                drop = weighted_rows(spread(following, at), full)
                if inverted[q]:
                    following = jnp.where(inside, 0.0, following)
                    left = jnp.where((wide >= at) & (wide < at + 8), 0.0, left)
                ahead[q] = following - drop
                matrices[q] = left - thin_product(done, done)
    return [jnp.concatenate(p, axis=0) for p in panels]


def multiply(left, right):
    return jnp.dot(left, right, precision=HIGHEST, preferred_element_type=F32)


def multiply_tn(left, right):
    return lax.dot_general(
        left, right, (((0,), (0,)), ((), ())), precision=HIGHEST, preferred_element_type=F32
    )


def covariance(row_x, row_y, col_x, col_y):
    dx = col_x - row_x
    dy = col_y - row_y
    return jnp.exp(-jnp.sqrt(dx * dx + dy * dy) / length_scale)


def build_covariances(slot_ref, there_ref, coords_ref, near_ref, cov):
    eye = (iota((B, B), 0) == iota((B, B), 1)).astype(F32)
    for q in range(2):
        own = coords_ref[slot_ref[q]]
        points = [
            (near_ref[0, q * K + k : q * K + k + 1, :], near_ref[1, q * K + k : q * K + k + 1, :])
            for k in range(K)
        ] + [(own[0:1], own[1:2])]
        there = [there_ref[q * K + k].astype(F32) for k in range(K)] + [jnp.float32(1.0)]
        for a in range(K + 1):
            col_x = jnp.broadcast_to(points[a][0], (B, B)).T
            col_y = jnp.broadcast_to(points[a][1], (B, B)).T
            for b in range(a, K + 1):
                block = covariance(points[b][0], points[b][1], col_x, col_y) * (there[a] * there[b])
                if a == b:
                    block = block + (nugget_var * there[a] + (1.0 - there[a])) * eye
                cov[q, a, :, b * B : (b + 1) * B] = block


def sample_kernel(
    key_ref,
    rank_ref,
    out_key_ref,
    slot_ref,
    there_ref,
    coords_ref,
    near_ref,
    draws_ref,
    out_ref,
    cov,
    inverses,
    weights,
    first_noise,
    noise,
    near_first,
    early,
    late,
    got_first,
    got_noise,
    got_later,
    got_near,
    values,
    turned,
    got_line,
    held,
    picked,
    got_cross,
    high,
    low,
    local_sem,
    col_send,
    col_recv,
    line_send,
    line_recv,
    cross_send,
    cross_recv,
):
    core, along, across = place()
    answers = greet(core, along, across)
    col = lax.axis_index("col")
    cols = lax.axis_size("col")
    peers = [(col + d) % cols for d in range(1, cols)]
    my_slot = 2 * along + core
    sub = iota((8, B), 0)
    rows = draws_ref.shape[0] * draws_ref.shape[1]
    draws = draws_ref[...].reshape(rows, B)
    held[ZERO_TILE] = jnp.zeros((8, B), F32)

    def to_peers(source, target, which):
        for to in peers:
            remote(source(to), target.at[col], col_send.at[which], col_recv.at[which], {"col": to}).start()

    def from_peers(target, sems, which):
        wait_bytes(target.at[pl.ds(0, cols - 1)], sems.at[which])

    def noise_of(section, tiles_ref):
        tiles = []
        for slot in range(CAP):
            rank = jnp.maximum(rank_ref[CAP * section + slot], 0)
            tile = tiles_ref[rank % cols]
            swapped = pltpu.roll(tile, 4, 0)
            keep = (rank // cols == slot).astype(F32)
            tiles.append(tile * keep + swapped * (1.0 - keep))
        return jnp.where(sub < 4, tiles[0], tiles[1])

    def spread_values(s, tile):
        values[s] = tile
        turned[CAP * s] = tile
        turned[CAP * s + 1] = pltpu.roll(tile, 4, 0)

    def prepare(section, both):
        for slot in range(CAP):
            rank = jnp.maximum(rank_ref[CAP * section + slot], 0)
            place_in_wave = rank % cols
            weight = early[place_in_wave]
            if both:
                is_late = (rank // cols).astype(F32)
                weight = weight * (1.0 - is_late) + late[place_in_wave] * is_late
            part = weight.astype(BF16)
            high[:, slot * B : (slot + 1) * B] = part
            low[:, slot * B : (slot + 1) * B] = (weight - part.astype(F32)).astype(BF16)

    def share(s):
        for device, slot in line_targets(core, along, across):
            remote(
                values.at[s], got_line.at[s, slot], line_send.at[s], line_recv.at[s], {"blk": device}
            ).start()
        got_line[s, my_slot] = values[s]

    def pass_on(s):
        wait_bytes(got_line.at[s, pl.ds(0, 2 * LINE - 1)], line_recv.at[s])
        first = s * (2 * LINE * CAP)
        for dev in range(2 * LINE):
            tile = got_line[s, dev]
            held[first + 2 * dev] = tile
            held[first + 2 * dev + 1] = pltpu.roll(tile, 4, 0)

        def pick(peer, slot_there):
            lanes = (s + 1) * (CAP * K)
            for k in range(K):
                upper = held[key_ref[peer, lanes + k]]
                lower = held[key_ref[peer, lanes + K + k]]
                slot_there[k] = jnp.where(sub < 4, upper, lower)

        for device, peer in cross_peers(core, along, across):
            pick(peer, picked.at[s, peer])
            remote(
                picked.at[s, peer], got_cross.at[s, across], cross_send.at[s], cross_recv.at[s], {"blk": device}
            ).start()
        pick(across, got_cross.at[s, across])

    def collect(s):
        wait_bytes(got_cross.at[s, pl.ds(0, LINE - 1)], cross_recv.at[s])
        near = []
        for k in range(K):
            tiles = [got_cross[s, peer, k] for peer in range(LINE)]
            while len(tiles) > 1:
                tiles = [tiles[i] + tiles[i + 1] for i in range(0, len(tiles), 2)]
            near.append(tiles[0])
        return jnp.concatenate(near, axis=1)

    def update(s, near, noise_now):
        part = near.astype(BF16).astype(F32)
        both = jnp.concatenate([part, near - part], axis=0).astype(BF16)
        first = jnp.dot(both, high[...], preferred_element_type=F32)
        second = jnp.dot(both[0:8], low[...], preferred_element_type=F32)
        total = first[0:8] + (first[8:16] + second)
        added = jnp.where(sub < 4, total[:, :B], total[:, B:])
        spread_values(s, added + noise_now)

    build_covariances(slot_ref, there_ref, coords_ref, near_ref, cov)
    def follow(q, k, inverse):
        rest = slice((k + 1) * B, (K + 1) * B)
        white = multiply(inverse, cov[q, k, :, rest])
        cov[q, k, :, rest] = white
        for row in range(k + 1, K + 1):
            first = (row - k - 1) * B
            cov[q, row, :, row * B :] = cov[q, row, :, row * B :] - multiply_tn(
                white[:, first : first + B], white[:, first:]
            )

    def back(q):
        for k in reversed(range(K)):
            total = cov[q, k, :, K * B :]
            if k + 1 < K:
                total = total - multiply(cov[q, k, :, (k + 1) * B : K * B], weights[q, (k + 1) * B :, :])
            weights[q, k * B : (k + 1) * B, :] = multiply_tn(inverses[q, k], total)

    def send_weights(q, buffer):
        to_peers(lambda to: weights.at[q], buffer, 4 + q)
        pltpu.make_async_copy(weights.at[q], buffer.at[col], local_sem.at[q]).start()

    def await_weights(q, buffer):
        from_peers(buffer, col_recv, 4 + q)
        pltpu.make_async_copy(weights.at[q], buffer.at[col], local_sem.at[q]).wait()

    def send_noise(q, rows_now):
        noise[q] = rows_now.reshape(noise.shape[1:])
        target = (got_noise, got_later)[q]
        to_peers(lambda to: noise.at[q, to], target, 2 + q)
        target[col] = noise[q, col]

    inverse, first_upper = panel_factors([cov[0, 0, :, :B], cov[0, K, :, K * B :]], [True, False])
    inverses[0, 0] = inverse
    first_noise[...] = multiply(draws, first_upper).reshape(first_noise.shape)
    await_answers(answers)
    to_peers(lambda to: first_noise.at[to], got_first, 0)
    got_first[col] = first_noise[col]
    follow(0, 0, inverse)

    def step(k, carry):
        start = pl.multiple_of(k * B, B)
        behind = pl.multiple_of((k - 1) * B, B)
        inverse = panel_factors(
            [cov[0, k, :, pl.ds(start, B)], cov[1, k - 1, :, pl.ds(behind, B)]], [True, True]
        )
        inverses[0, k] = inverse[0]
        inverses[1, k - 1] = inverse[1]
        for at in range(1, K):

            @pl.when(k == at)
            def _(at=at):
                follow(0, at, inverse[0])
                follow(1, at - 1, inverse[1])
                if at == 1:
                    from_peers(got_first, col_recv, 0)
                    spread_values(0, noise_of(0, got_first))
                    share(0)
                elif at == 2:
                    pass_on(0)
                else:
                    near_first[...] = collect(0)
                    to_peers(lambda to: near_first, got_near, 1)
                    got_near[col] = near_first[...]

        return carry

    lax.fori_loop(1, K, step, 0)
    inverse, upper = panel_factors([cov[1, K - 1, :, (K - 1) * B : K * B], cov[0, K, :, K * B :]], [True, False])
    inverses[1, K - 1] = inverse
    back(0)
    drawn = multiply(draws, upper)
    from_peers(got_near, col_recv, 1)
    near = got_near[...].reshape(rows, K * B)
    near_slots = [near, pltpu.roll(near, rows - 4, 0)]
    chosen = jnp.zeros((rows, K * B), F32)
    for slot in range(CAP):
        chosen = chosen + near_slots[slot] * (rank_ref[CAP + slot] == col).astype(F32)
    send_noise(0, drawn + multiply(chosen, weights[0]))
    send_weights(0, early)
    from_peers(got_noise, col_recv, 2)
    spread_values(1, noise_of(1, got_noise))
    share(1)
    follow(1, K - 1, inverses[1, K - 1])
    upper = panel_factors([cov[1, K, :, K * B :]], [False])[0]
    pass_on(1)
    back(1)
    send_noise(1, multiply(draws, upper))
    send_weights(1, late)
    await_weights(0, early)
    prepare(2, False)
    update(2, collect(1), noise_of(2, got_noise))
    share(2)
    pass_on(2)
    from_peers(got_later, col_recv, 3)
    for owner in range(cols):
        got_first[owner] = jnp.where(sub < 4, got_noise[owner], got_later[owner])
    await_weights(1, late)
    prepare(3, True)
    update(3, collect(2), noise_of(3, got_first))
    share(3)

    def section(s, carry):
        prepare(s + 1, True)
        pass_on(s)
        update(s + 1, collect(s), noise_of(s + 1, got_first))

        @pl.when(s + 1 < ROUNDS)
        def _():
            share(s + 1)

        return carry

    lax.fori_loop(3, ROUNDS, section, 0)
    for block in range(out_ref.shape[1] // B):
        out_ref[:, block * B : (block + 1) * B] = turned[out_key_ref[block]][0:4]
    from_peers(got_first, col_send, 0)
    from_peers(got_near, col_send, 1)
    from_peers(got_noise, col_send, 2)
    from_peers(got_later, col_send, 3)
    from_peers(early, col_send, 4)
    from_peers(late, col_send, 5)

    def finish(s, carry):
        wait_bytes(got_line.at[s, pl.ds(0, 2 * LINE - 1)], line_send.at[s])
        wait_bytes(got_cross.at[s, pl.ds(0, LINE - 1)], cross_send.at[s])
        return carry

    lax.fori_loop(0, ROUNDS, finish, 0)


VMEM_SPEC = pl.BlockSpec(memory_space=pltpu.VMEM)
SMEM_SPEC = pl.BlockSpec(memory_space=pltpu.SMEM)
VMEM_LIMIT = 40 * 1024 * 1024


def local(coords, neighbours, sections, normals):
    cols = lax.axis_size("col")
    i32 = jnp.int32
    shape = jax.ShapeDtypeStruct
    near, key, draws, rank_of_cell, out_key, my_slots, there = pl.pallas_call(
        exchange_kernel,
        out_shape=(
            shape((2, 8, B), F32),
            shape((LINE, B), i32),
            shape((cols, 8, B), F32),
            shape((SECTIONS * CAP,), i32),
            shape((LINE,), i32),
            shape((2,), i32),
            shape((2 * K,), i32),
        ),
        in_specs=[SMEM_SPEC] * 2 + [VMEM_SPEC] * 2,
        out_specs=(VMEM_SPEC,) * 3 + (SMEM_SPEC,) * 4,
        scratch_shapes=[
            pltpu.VMEM((3, 8, B), F32),
            pltpu.VMEM((2, 8, B), i32),
            pltpu.VMEM((cols, 8, B), F32),
            pltpu.VMEM((2 * LINE, 3, 8, B), F32),
            pltpu.VMEM((LINE, 2, 8, B), i32),
            pltpu.VMEM((cols, 8, B), F32),
            pltpu.VMEM((LINE, 2, 8, B), F32),
            pltpu.VMEM((LINE, 2, 8, B), F32),
            pltpu.SemaphoreType.DMA((4,)),
            pltpu.SemaphoreType.DMA((4,)),
        ],
        compiler_params=pltpu.CompilerParams(
            collective_id=0, has_side_effects=True, vmem_limit_bytes=VMEM_LIMIT
        ),
        name="exchange",
    )(sections, neighbours, coords, normals)

    return pl.pallas_call(
        sample_kernel,
        out_shape=shape(normals.shape, F32),
        in_specs=[SMEM_SPEC] * 5 + [VMEM_SPEC] * 3,
        out_specs=VMEM_SPEC,
        scratch_shapes=[
            pltpu.VMEM((2, K + 1, B, (K + 1) * B), F32),
            pltpu.VMEM((2, K, B, B), F32),
            pltpu.VMEM((2, K * B, B), F32),
            pltpu.VMEM((cols, 8, B), F32),
            pltpu.VMEM((2, cols, 8, B), F32),
            pltpu.VMEM((8, K * B), F32),
            pltpu.VMEM((cols, K * B, B), F32),
            pltpu.VMEM((cols, K * B, B), F32),
            pltpu.VMEM((cols, 8, B), F32),
            pltpu.VMEM((cols, 8, B), F32),
            pltpu.VMEM((cols, 8, B), F32),
            pltpu.VMEM((cols, 8, K * B), F32),
            pltpu.VMEM((SECTIONS, 8, B), F32),
            pltpu.VMEM((SECTIONS * CAP, 8, B), F32),
            pltpu.VMEM((ROUNDS, 2 * LINE, 8, B), F32),
            pltpu.VMEM((ZERO_TILE + 1, 8, B), F32),
            pltpu.VMEM((ROUNDS, LINE, K, 8, B), F32),
            pltpu.VMEM((ROUNDS, LINE, K, 8, B), F32),
            pltpu.VMEM((K * B, CAP * B), BF16),
            pltpu.VMEM((K * B, CAP * B), BF16),
            pltpu.SemaphoreType.DMA((2,)),
            pltpu.SemaphoreType.DMA((6,)),
            pltpu.SemaphoreType.DMA((6,)),
            pltpu.SemaphoreType.DMA((ROUNDS,)),
            pltpu.SemaphoreType.DMA((ROUNDS,)),
            pltpu.SemaphoreType.DMA((ROUNDS,)),
            pltpu.SemaphoreType.DMA((ROUNDS,)),
        ],
        compiler_params=pltpu.CompilerParams(
            collective_id=1, has_side_effects=True, vmem_limit_bytes=VMEM_LIMIT
        ),
        name="sample",
    )(key, rank_of_cell, out_key, my_slots, there, coords, near, draws)


def solution(mesh):
    in_specs = (P("blk", None, None), P("blk", None), P("blk"), P("col", "blk"))
    out_specs = P("col", "blk")
    return jax.shard_map(local, mesh=mesh, in_specs=in_specs, out_specs=out_specs, check_vma=False)
```

```python
import jax
import jax.numpy as jnp
from jax import lax
from jax.experimental import pallas as pl
from jax.experimental.pallas import tpu as pltpu
from jax.sharding import PartitionSpec as P

K = 4
SECTIONS = 8
CAP = 2
B = 128
ROUNDS = SECTIONS - 1
LINE = 8
ZERO_TILE = ROUNDS * 2 * LINE * CAP

length_scale = 0.5
nugget_var = 0.1

HIGHEST = lax.Precision.HIGHEST
F32 = jnp.float32
BF16 = jnp.bfloat16


def iota(shape, dim):
    return lax.broadcasted_iota(jnp.int32, shape, dim)


def place():
    blk = lax.axis_index("blk")
    core = blk % 2
    y = (blk // 2) % LINE
    z = blk // (2 * LINE)
    along = (1 - core) * z + core * y
    across = (1 - core) * y + core * z
    return core, along, across


def device_at(core, along, across, other_core):
    chip = (1 - core) * (along * LINE + across) + core * (across * LINE + along)
    return chip * 2 + other_core


FAR_FIRST = (4, 3, 5, 2, 6, 1, 7)


def line_targets(core, along, across):
    targets = []
    for d in FAR_FIRST + (0,):
        if d:
            targets.append((device_at(core, (along + d) % LINE, across, core), 2 * along + core))
        targets.append((device_at(core, along, (across + d) % LINE, 1 - core), 2 * across + core))
    return targets


def line_sources(core, along, across):
    same = [device_at(core, (along + d) % LINE, across, core) for d in range(1, LINE)]
    other = [device_at(core, (along + d) % LINE, across, 1 - core) for d in range(LINE)]
    return same + other


def cross_peers(core, along, across):
    return [
        (device_at(core, along, (across + d) % LINE, core), (across + d) % LINE) for d in FAR_FIRST
    ]


def greet(core, along, across):
    barrier = pltpu.get_barrier_semaphore()
    col = lax.axis_index("col")
    cols = lax.axis_size("col")
    mesh_id = pl.DeviceIdType.MESH
    sources = line_sources(core, along, across) + [device for device, _ in cross_peers(core, along, across)]
    for device in sources:
        pl.semaphore_signal(barrier, inc=1, device_id={"blk": device}, device_id_type=mesh_id)
    for d in range(1, cols):
        pl.semaphore_signal(barrier, inc=1, device_id={"col": (col + d) % cols}, device_id_type=mesh_id)
    return len(sources) + cols - 1


def await_answers(count):
    pl.semaphore_wait(pltpu.get_barrier_semaphore(), count)


def remote(src, dst, send_sem, recv_sem, device_id):
    return pltpu.make_async_remote_copy(
        src_ref=src,
        dst_ref=dst,
        send_sem=send_sem,
        recv_sem=recv_sem,
        device_id=device_id,
        device_id_type=pl.DeviceIdType.MESH,
    )


def wait_bytes(ref, sem):
    pltpu.make_async_copy(ref, ref, sem).wait()


def exchange_kernel(
    sections_ref,
    neighbours_ref,
    coords_hbm,
    normals_hbm,
    near_ref,
    key_ref,
    draws_ref,
    rank_ref,
    out_key_ref,
    there_ref,
    own_a,
    own_b,
    own_n,
    got_a,
    got_b,
    got_n,
    picked,
    got_p,
    coords_ref,
    normals_ref,
    send_sems,
    recv_sems,
    local_sems,
):
    core, along, across = place()
    answers = greet(core, along, across)
    loads = [
        pltpu.make_async_copy(coords_hbm, coords_ref, local_sems.at[0]),
        pltpu.make_async_copy(normals_hbm, normals_ref, local_sems.at[1]),
    ]
    for load in loads:
        load.start()
    col = lax.axis_index("col")
    cols = lax.axis_size("col")
    my_slot = 2 * along + core
    sub, lane = iota((8, B), 0), iota((8, B), 1)
    blocks = range(LINE)

    def flag(condition):
        return condition.astype(jnp.int32)

    section = [sections_ref[i] for i in blocks]
    listed = [[neighbours_ref[i, k] for k in range(K)] for i in blocks]
    within = [sum((flag(section[j] == section[i]) for j in range(i)), jnp.int32(0)) for i in blocks]
    rank = [within[i] + sum(flag(section[j] < section[i]) for j in blocks) for i in blocks]
    cell = [section[i] * CAP + within[i] for i in blocks]
    for c in range(SECTIONS * CAP):
        rank_ref[c] = sum(flag(cell[i] == c) * (rank[i] + 1) for i in blocks) - 1
    code = jnp.zeros((8, B), F32)
    asked = jnp.full((8, B), -1, jnp.int32)
    for i in blocks:
        out_key_ref[i] = cell[i]
        code = jnp.where(sub == i, (section[i] * (2 * LINE * CAP) + within[i]).astype(F32), code)
        for k in range(K):
            asked = jnp.where(lane == cell[i] * K + k, listed[i][k], asked)
    ids = jnp.full((8, B), -1, jnp.int32)
    slots = []
    for half in range(2):
        mine = [flag(rank[i] == col + half * cols) for i in blocks]
        slots.append(sum(mine[i] * i for i in blocks))
        for k in range(K):
            entry = sum(mine[i] * (listed[i][k] + 1) for i in blocks) - 1
            there_ref[half * K + k] = flag(entry >= 0)
            ids = jnp.where(sub == half * K + k, entry, ids)
    loads[0].wait()
    own_a[0] = coords_ref[:, 0, :]
    own_a[1] = coords_ref[:, 1, :]
    own_a[2] = code
    for axis in range(2):
        chosen = [
            jnp.sum(jnp.where(sub == slots[half], own_a[axis], 0.0), axis=0, keepdims=True) for half in range(2)
        ]
        near_ref[axis, 8:16, :] = jnp.where(sub == 0, chosen[0], chosen[1])
    own_b[0] = ids
    own_b[1] = asked
    loads[1].wait()
    for owner in range(cols):
        for half in range(2):
            drawn = jnp.zeros((4, B), F32)
            for i in blocks:
                chosen = (rank[i] == owner + half * cols).astype(F32)
                drawn = drawn + normals_ref[:, i * B : (i + 1) * B] * chosen
            own_n[owner, half * 4 : half * 4 + 4, :] = drawn
    await_answers(answers)
    for device, slot in line_targets(core, along, across):
        remote(own_a, got_a.at[slot], send_sems.at[0], recv_sems.at[0], {"blk": device}).start()
    for device, _ in cross_peers(core, along, across):
        remote(own_b, got_b.at[across], send_sems.at[1], recv_sems.at[1], {"blk": device}).start()
    for d in range(1, cols):
        to = (col + d) % cols
        remote(own_n.at[to], got_n.at[col], send_sems.at[2], recv_sems.at[2], {"col": to}).start()
    got_a[my_slot] = own_a[...]
    got_b[across] = own_b[...]
    got_n[col] = own_n[col]
    lane = iota((1, B), 1)
    lane_dev = device_at(core, lane // (2 * LINE), across, (lane // LINE) % 2)
    lane_block = lane_dev * LINE + lane % LINE
    sub = iota((LINE, B), 0)
    entry_half = (iota((1, B), 1) // K) % 2
    wait_bytes(got_a.at[pl.ds(0, 2 * LINE - 1)], recv_sems.at[0])
    wait_bytes(got_b.at[pl.ds(0, LINE - 1)], recv_sems.at[1])
    chosen = jnp.concatenate(
        [(got_b[peer, 0] == lane_block).astype(F32) for peer in range(LINE)], axis=0
    )
    for axis in range(2):
        held = got_a[:, axis].reshape(B, B)
        moved = jnp.dot(chosen, held, precision=HIGHEST, preferred_element_type=F32)
        picked[:, axis] = moved.reshape(LINE, LINE, B)
    for device, peer in cross_peers(core, along, across):
        remote(picked.at[peer], got_p.at[across], send_sems.at[3], recv_sems.at[3], {"blk": device}).start()
    got_p[across] = picked[across]
    sums = [jnp.zeros((LINE, B), jnp.int32) for _ in range(LINE)]
    for dev in range(2 * LINE):
        block = device_at(core, dev // 2, across, dev % 2) * LINE + sub
        value = got_a[dev, 2].astype(jnp.int32) + (2 * dev + 1)
        for peer in range(LINE):
            sums[peer] = sums[peer] + jnp.where(block == got_b[peer, 1], value, 0)
    for peer in range(LINE):
        total = jnp.sum(sums[peer], axis=0, keepdims=True)
        value = total - 1
        turned = value + entry_half * (1 - 2 * (value % 2))
        key_ref[peer : peer + 1, :] = jnp.where(total > 0, turned, ZERO_TILE)
    wait_bytes(got_n.at[pl.ds(0, cols - 1)], recv_sems.at[2])
    draws_ref[...] = got_n[...]
    wait_bytes(got_p.at[pl.ds(0, LINE - 1)], recv_sems.at[3])
    for axis in range(2):
        near = got_p[0, axis]
        for peer in range(1, LINE):
            near = near + got_p[peer, axis]
        near_ref[axis, 0:8, :] = near
    wait_bytes(got_a.at[pl.ds(0, 2 * LINE - 1)], send_sems.at[0])
    wait_bytes(got_b.at[pl.ds(0, LINE - 1)], send_sems.at[1])
    wait_bytes(got_n.at[pl.ds(0, cols - 1)], send_sems.at[2])
    wait_bytes(got_p.at[pl.ds(0, LINE - 1)], send_sems.at[3])


def split3(x):
    high = x.astype(BF16).astype(F32)
    rest = x - high
    middle = rest.astype(BF16).astype(F32)
    return high, middle, rest - middle


def thin_product(left, right):
    l1, l2, l3 = split3(left)
    r1, r2, r3 = split3(right)
    tall_left = jnp.concatenate([l1, l1, l2, l2, l1, l3], axis=0).astype(BF16)
    tall_right = jnp.concatenate([r1, r2, r1, r2, r3, r1], axis=0).astype(BF16)
    return lax.dot_general(tall_left, tall_right, (((0,), (0,)), ((), ())), preferred_element_type=F32)


def spread(tile, first):
    return [jnp.take_along_axis(tile, jnp.full((8, B), first + j, jnp.int32), axis=1) for j in range(8)]


def weighted_rows(factors, rows):
    terms = [factors[j] * rows[j : j + 1, :] for j in range(8)]
    return ((terms[0] + terms[1]) + (terms[2] + terms[3])) + ((terms[4] + terms[5]) + (terms[6] + terms[7]))


def eliminate(rows, columns, sub):
    columns = list(columns)
    full = rows
    scales = []
    for j in range(8):
        below, here = sub > j, sub == j
        pivot = columns[j][j : j + 1, :]
        inverse = 1.0 / pivot
        factors = columns[j] * inverse
        under = jnp.where(below, factors, 0.0)
        scaled = full[j : j + 1, :] * inverse
        full = jnp.where(here, scaled, full - columns[j] * scaled)
        rows = rows - under * rows[j : j + 1, :]
        for later in range(j + 1, 8):
            columns[later] = jnp.where(
                here, columns[later] * inverse, columns[later] - factors * columns[later][j : j + 1, :]
            )
        scales.append(lax.rsqrt(pivot))
    scale = scales[7]
    for j in range(7):
        scale = jnp.where(sub == j, scales[j], scale)
    return rows * scale, full


def panel_factors(matrices, inverted):
    sub, lane = iota((8, B), 0), iota((8, B), 1)
    wide = iota((B, B), 1)
    matrices = list(matrices)
    ahead = [m[0:8] for m in matrices]
    panels = [[] for _ in matrices]
    for panel in range(B // 8):
        at = 8 * panel
        inside = (lane >= at) & (lane < at + 8)
        for q in range(len(matrices)):
            rows, left = ahead[q], matrices[q]
            if inverted[q]:
                unit = jnp.where(lane == sub + at, 1.0, 0.0)
                done, full = eliminate(jnp.where(inside, unit, rows), spread(rows, at), sub)
                panels[q].append(jnp.where(lane < at + 8, done, 0.0))
            else:
                done, full = eliminate(rows, spread(rows, at), sub)
                panels[q].append(jnp.where(lane >= sub + at, done, 0.0))
            if at + 8 < B:
                following = left[at + 8 : at + 16]
                drop = weighted_rows(spread(following, at), full)
                if inverted[q]:
                    following = jnp.where(inside, 0.0, following)
                    left = jnp.where((wide >= at) & (wide < at + 8), 0.0, left)
                ahead[q] = following - drop
                matrices[q] = left - thin_product(done, done)
    return [jnp.concatenate(p, axis=0) for p in panels]


def multiply(left, right):
    return jnp.dot(left, right, precision=HIGHEST, preferred_element_type=F32)


def multiply_tn(left, right):
    return lax.dot_general(
        left, right, (((0,), (0,)), ((), ())), precision=HIGHEST, preferred_element_type=F32
    )


def covariance(row_x, row_y, col_x, col_y):
    dx = col_x - row_x
    dy = col_y - row_y
    return jnp.exp(-jnp.sqrt(dx * dx + dy * dy) / length_scale)


def build_covariances(there_ref, near_ref, cov):
    eye = (iota((B, B), 0) == iota((B, B), 1)).astype(F32)
    for q in range(2):
        points = [
            (near_ref[0, q * K + k : q * K + k + 1, :], near_ref[1, q * K + k : q * K + k + 1, :])
            for k in range(K)
        ] + [(near_ref[0, 8 + q : 9 + q, :], near_ref[1, 8 + q : 9 + q, :])]
        there = [there_ref[q * K + k].astype(F32) for k in range(K)] + [jnp.float32(1.0)]
        for a in range(K + 1):
            col_x = jnp.broadcast_to(points[a][0], (B, B)).T
            col_y = jnp.broadcast_to(points[a][1], (B, B)).T
            for b in range(a, K + 1):
                block = covariance(points[b][0], points[b][1], col_x, col_y) * (there[a] * there[b])
                if a == b:
                    block = block + (nugget_var * there[a] + (1.0 - there[a])) * eye
                cov[q, a, :, b * B : (b + 1) * B] = block


def sample_kernel(
    key_ref,
    rank_ref,
    out_key_ref,
    there_ref,
    near_ref,
    draws_ref,
    out_ref,
    cov,
    inverses,
    weights,
    first_noise,
    noise,
    near_first,
    early,
    late,
    got_first,
    got_noise,
    got_later,
    got_near,
    values,
    turned,
    got_line,
    held,
    picked,
    got_cross,
    high,
    low,
    local_sem,
    col_send,
    col_recv,
    line_send,
    line_recv,
    cross_send,
    cross_recv,
):
    core, along, across = place()
    answers = greet(core, along, across)
    col = lax.axis_index("col")
    cols = lax.axis_size("col")
    peers = [(col + d) % cols for d in range(1, cols)]
    my_slot = 2 * along + core
    sub = iota((8, B), 0)
    rows = draws_ref.shape[0] * draws_ref.shape[1]
    draws = draws_ref[...].reshape(rows, B)
    held[ZERO_TILE] = jnp.zeros((8, B), F32)

    def to_peers(source, target, which):
        for to in peers:
            remote(source(to), target.at[col], col_send.at[which], col_recv.at[which], {"col": to}).start()

    def from_peers(target, sems, which):
        wait_bytes(target.at[pl.ds(0, cols - 1)], sems.at[which])

    def noise_of(section, tiles_ref):
        tiles = []
        for slot in range(CAP):
            rank = jnp.maximum(rank_ref[CAP * section + slot], 0)
            tile = tiles_ref[rank % cols]
            swapped = pltpu.roll(tile, 4, 0)
            keep = (rank // cols == slot).astype(F32)
            tiles.append(tile * keep + swapped * (1.0 - keep))
        return jnp.where(sub < 4, tiles[0], tiles[1])

    def spread_values(s, tile):
        values[s] = tile
        turned[CAP * s] = tile
        turned[CAP * s + 1] = pltpu.roll(tile, 4, 0)

    def prepare(section, both):
        for slot in range(CAP):
            rank = jnp.maximum(rank_ref[CAP * section + slot], 0)
            place_in_wave = rank % cols
            weight = early[place_in_wave]
            if both:
                is_late = (rank // cols).astype(F32)
                weight = weight * (1.0 - is_late) + late[place_in_wave] * is_late
            part = weight.astype(BF16)
            high[:, slot * B : (slot + 1) * B] = part
            low[:, slot * B : (slot + 1) * B] = (weight - part.astype(F32)).astype(BF16)

    def share(s):
        for device, slot in line_targets(core, along, across):
            remote(
                values.at[s], got_line.at[s, slot], line_send.at[s], line_recv.at[s], {"blk": device}
            ).start()
        got_line[s, my_slot] = values[s]

    def pass_on(s):
        wait_bytes(got_line.at[s, pl.ds(0, 2 * LINE - 1)], line_recv.at[s])
        first = s * (2 * LINE * CAP)
        for dev in range(2 * LINE):
            tile = got_line[s, dev]
            held[first + 2 * dev] = tile
            held[first + 2 * dev + 1] = pltpu.roll(tile, 4, 0)

        def pick(peer, slot_there):
            lanes = (s + 1) * (CAP * K)
            for k in range(K):
                upper = held[key_ref[peer, lanes + k]]
                lower = held[key_ref[peer, lanes + K + k]]
                slot_there[k] = jnp.where(sub < 4, upper, lower)

        for device, peer in cross_peers(core, along, across):
            pick(peer, picked.at[s, peer])
            remote(
                picked.at[s, peer], got_cross.at[s, across], cross_send.at[s], cross_recv.at[s], {"blk": device}
            ).start()
        pick(across, got_cross.at[s, across])

    def collect(s):
        wait_bytes(got_cross.at[s, pl.ds(0, LINE - 1)], cross_recv.at[s])
        near = []
        for k in range(K):
            tiles = [got_cross[s, peer, k] for peer in range(LINE)]
            while len(tiles) > 1:
                tiles = [tiles[i] + tiles[i + 1] for i in range(0, len(tiles), 2)]
            near.append(tiles[0])
        return jnp.concatenate(near, axis=1)

    def update(s, near, noise_now):
        part = near.astype(BF16).astype(F32)
        both = jnp.concatenate([part, near - part], axis=0).astype(BF16)
        first = jnp.dot(both, high[...], preferred_element_type=F32)
        second = jnp.dot(both[0:8], low[...], preferred_element_type=F32)
        total = first[0:8] + (first[8:16] + second)
        added = jnp.where(sub < 4, total[:, :B], total[:, B:])
        spread_values(s, added + noise_now)

    build_covariances(there_ref, near_ref, cov)
    def follow(q, k, inverse):
        rest = slice((k + 1) * B, (K + 1) * B)
        white = multiply(inverse, cov[q, k, :, rest])
        cov[q, k, :, rest] = white
        for row in range(k + 1, K + 1):
            first = (row - k - 1) * B
            cov[q, row, :, row * B :] = cov[q, row, :, row * B :] - multiply_tn(
                white[:, first : first + B], white[:, first:]
            )

    def back(q):
        for k in reversed(range(K)):
            total = cov[q, k, :, K * B :]
            if k + 1 < K:
                total = total - multiply(cov[q, k, :, (k + 1) * B : K * B], weights[q, (k + 1) * B :, :])
            weights[q, k * B : (k + 1) * B, :] = multiply_tn(inverses[q, k], total)

    def send_weights(q, buffer):
        to_peers(lambda to: weights.at[q], buffer, 4 + q)
        pltpu.make_async_copy(weights.at[q], buffer.at[col], local_sem.at[q]).start()

    def await_weights(q, buffer):
        from_peers(buffer, col_recv, 4 + q)
        pltpu.make_async_copy(weights.at[q], buffer.at[col], local_sem.at[q]).wait()

    def send_noise(q, rows_now):
        noise[q] = rows_now.reshape(noise.shape[1:])
        target = (got_noise, got_later)[q]
        to_peers(lambda to: noise.at[q, to], target, 2 + q)
        target[col] = noise[q, col]

    inverse, first_upper = panel_factors([cov[0, 0, :, :B], cov[0, K, :, K * B :]], [True, False])
    inverses[0, 0] = inverse
    first_noise[...] = multiply(draws, first_upper).reshape(first_noise.shape)
    await_answers(answers)
    to_peers(lambda to: first_noise.at[to], got_first, 0)
    got_first[col] = first_noise[col]
    follow(0, 0, inverse)

    def step(k, carry):
        start = pl.multiple_of(k * B, B)
        behind = pl.multiple_of((k - 1) * B, B)
        inverse = panel_factors(
            [cov[0, k, :, pl.ds(start, B)], cov[1, k - 1, :, pl.ds(behind, B)]], [True, True]
        )
        inverses[0, k] = inverse[0]
        inverses[1, k - 1] = inverse[1]
        for at in range(1, K):

            @pl.when(k == at)
            def _(at=at):
                follow(0, at, inverse[0])
                follow(1, at - 1, inverse[1])
                if at == 1:
                    from_peers(got_first, col_recv, 0)
                    spread_values(0, noise_of(0, got_first))
                    share(0)
                elif at == 2:
                    pass_on(0)
                else:
                    near_first[...] = collect(0)
                    to_peers(lambda to: near_first, got_near, 1)
                    got_near[col] = near_first[...]

        return carry

    lax.fori_loop(1, K, step, 0)
    inverse, upper = panel_factors([cov[1, K - 1, :, (K - 1) * B : K * B], cov[0, K, :, K * B :]], [True, False])
    inverses[1, K - 1] = inverse
    back(0)
    drawn = multiply(draws, upper)
    from_peers(got_near, col_recv, 1)
    near = got_near[...].reshape(rows, K * B)
    near_slots = [near, pltpu.roll(near, rows - 4, 0)]
    chosen = jnp.zeros((rows, K * B), F32)
    for slot in range(CAP):
        chosen = chosen + near_slots[slot] * (rank_ref[CAP + slot] == col).astype(F32)
    send_noise(0, drawn + multiply(chosen, weights[0]))
    send_weights(0, early)
    from_peers(got_noise, col_recv, 2)
    spread_values(1, noise_of(1, got_noise))
    share(1)
    follow(1, K - 1, inverses[1, K - 1])
    back(1)
    pass_on(1)
    send_weights(1, late)
    upper = panel_factors([cov[1, K, :, K * B :]], [False])[0]
    send_noise(1, multiply(draws, upper))
    await_weights(0, early)
    prepare(2, False)
    update(2, collect(1), noise_of(2, got_noise))
    share(2)
    pass_on(2)
    from_peers(got_later, col_recv, 3)
    for owner in range(cols):
        got_first[owner] = jnp.where(sub < 4, got_noise[owner], got_later[owner])
    await_weights(1, late)
    prepare(3, True)
    update(3, collect(2), noise_of(3, got_first))
    share(3)

    def section(s, carry):
        prepare(s + 1, True)
        pass_on(s)
        update(s + 1, collect(s), noise_of(s + 1, got_first))

        @pl.when(s + 1 < ROUNDS)
        def _():
            share(s + 1)

        return carry

    lax.fori_loop(3, ROUNDS, section, 0)
    for block in range(out_ref.shape[1] // B):
        out_ref[:, block * B : (block + 1) * B] = turned[out_key_ref[block]][0:4]
    from_peers(got_first, col_send, 0)
    from_peers(got_near, col_send, 1)
    from_peers(got_noise, col_send, 2)
    from_peers(got_later, col_send, 3)
    from_peers(early, col_send, 4)
    from_peers(late, col_send, 5)

    def finish(s, carry):
        wait_bytes(got_line.at[s, pl.ds(0, 2 * LINE - 1)], line_send.at[s])
        wait_bytes(got_cross.at[s, pl.ds(0, LINE - 1)], cross_send.at[s])
        return carry

    lax.fori_loop(0, ROUNDS, finish, 0)


VMEM_SPEC = pl.BlockSpec(memory_space=pltpu.VMEM)
SMEM_SPEC = pl.BlockSpec(memory_space=pltpu.SMEM)
VMEM_LIMIT = 40 * 1024 * 1024


def local(coords, neighbours, sections, normals):
    cols = lax.axis_size("col")
    i32 = jnp.int32
    shape = jax.ShapeDtypeStruct
    near, key, draws, rank_of_cell, out_key, there = pl.pallas_call(
        exchange_kernel,
        out_shape=(
            shape((2, 16, B), F32),
            shape((LINE, B), i32),
            shape((cols, 8, B), F32),
            shape((SECTIONS * CAP,), i32),
            shape((LINE,), i32),
            shape((2 * K,), i32),
        ),
        in_specs=[SMEM_SPEC] * 2 + [pl.BlockSpec(memory_space=pl.ANY)] * 2,
        out_specs=(VMEM_SPEC,) * 3 + (SMEM_SPEC,) * 3,
        scratch_shapes=[
            pltpu.VMEM((3, 8, B), F32),
            pltpu.VMEM((2, 8, B), i32),
            pltpu.VMEM((cols, 8, B), F32),
            pltpu.VMEM((2 * LINE, 3, 8, B), F32),
            pltpu.VMEM((LINE, 2, 8, B), i32),
            pltpu.VMEM((cols, 8, B), F32),
            pltpu.VMEM((LINE, 2, 8, B), F32),
            pltpu.VMEM((LINE, 2, 8, B), F32),
            pltpu.VMEM(coords.shape, F32),
            pltpu.VMEM(normals.shape, F32),
            pltpu.SemaphoreType.DMA((4,)),
            pltpu.SemaphoreType.DMA((4,)),
            pltpu.SemaphoreType.DMA((2,)),
        ],
        compiler_params=pltpu.CompilerParams(
            collective_id=0, has_side_effects=True, vmem_limit_bytes=VMEM_LIMIT
        ),
        name="exchange",
    )(sections, neighbours, coords, normals)

    return pl.pallas_call(
        sample_kernel,
        out_shape=shape(normals.shape, F32),
        in_specs=[SMEM_SPEC] * 4 + [VMEM_SPEC] * 2,
        out_specs=VMEM_SPEC,
        scratch_shapes=[
            pltpu.VMEM((2, K + 1, B, (K + 1) * B), F32),
            pltpu.VMEM((2, K, B, B), F32),
            pltpu.VMEM((2, K * B, B), F32),
            pltpu.VMEM((cols, 8, B), F32),
            pltpu.VMEM((2, cols, 8, B), F32),
            pltpu.VMEM((8, K * B), F32),
            pltpu.VMEM((cols, K * B, B), F32),
            pltpu.VMEM((cols, K * B, B), F32),
            pltpu.VMEM((cols, 8, B), F32),
            pltpu.VMEM((cols, 8, B), F32),
            pltpu.VMEM((cols, 8, B), F32),
            pltpu.VMEM((cols, 8, K * B), F32),
            pltpu.VMEM((SECTIONS, 8, B), F32),
            pltpu.VMEM((SECTIONS * CAP, 8, B), F32),
            pltpu.VMEM((ROUNDS, 2 * LINE, 8, B), F32),
            pltpu.VMEM((ZERO_TILE + 1, 8, B), F32),
            pltpu.VMEM((ROUNDS, LINE, K, 8, B), F32),
            pltpu.VMEM((ROUNDS, LINE, K, 8, B), F32),
            pltpu.VMEM((K * B, CAP * B), BF16),
            pltpu.VMEM((K * B, CAP * B), BF16),
            pltpu.SemaphoreType.DMA((2,)),
            pltpu.SemaphoreType.DMA((6,)),
            pltpu.SemaphoreType.DMA((6,)),
            pltpu.SemaphoreType.DMA((ROUNDS,)),
            pltpu.SemaphoreType.DMA((ROUNDS,)),
            pltpu.SemaphoreType.DMA((ROUNDS,)),
            pltpu.SemaphoreType.DMA((ROUNDS,)),
        ],
        compiler_params=pltpu.CompilerParams(
            collective_id=1, has_side_effects=True, vmem_limit_bytes=VMEM_LIMIT
        ),
        name="sample",
    )(key, rank_of_cell, out_key, there, near, draws)


def solution(mesh):
    in_specs = (P("blk", None, None), P("blk", None), P("blk"), P("col", "blk"))
    out_specs = P("col", "blk")
    return jax.shard_map(local, mesh=mesh, in_specs=in_specs, out_specs=out_specs, check_vma=False)
```
